256 devices in a mesh: section: 8 (over x, z_hi), dp: 16 (over z_lo, y), tensor: 2 (over core).
Axes of the slice: x: 4, y: 4, z: 8 (z_hi: 2, z_lo: 4; z = z_hi * 4 + z_lo), core: 2. Of those that a mesh axis runs over, the one named last changes fastest.
Arguments:
- section_inputs: bfloat16 [8, 4, 512, 8192], P('section', None, ('dp', 'tensor')), may hold values from -6 to 6
- top_grad: bfloat16 [4, 512, 8192], P(None, ('dp', 'tensor')), may hold values from -6 to 6
- value_weight: bfloat16 [8, 8192, 512], P('section', 'dp', 'tensor'), may hold values from -0.0625 to 0.0625
- output_weight: bfloat16 [8, 512, 8192], P('section', 'tensor', 'dp'), may hold values from -0.0625 to 0.0625
- owner_lengths: int32 [8, 2, 16], P('section', 'tensor'), may hold values from 196608 to 327680, as said below
- master_param: float32 [8, 2, 5242880], P('section', 'tensor', 'dp'), may hold values from -6 to 6
- moment1: float32 [8, 2, 5242880], P('section', 'tensor', 'dp'), may hold values from -4 to 4
- moment2: float32 [8, 2, 5242880], P('section', 'tensor', 'dp'), may hold values from 0.05 to 2
Outputs:
- input_grads: bfloat16 [8, 4, 512, 8192], P('section', None, ('dp', 'tensor'))
- new_param: float32 [8, 2, 5242880], P('section', 'tensor', 'dp')
- new_moment1: float32 [8, 2, 5242880], P('section', 'tensor', 'dp')
- new_moment2: float32 [8, 2, 5242880], P('section', 'tensor', 'dp')
The draws below stay inside these ranges and needn't reach their ends.
Inputs may be any that keep to these rules, and one draw needn't show every extreme that they name: `owner_lengths`: every row of 16 lengths sums to 4194304; owner d's range starts at d * 262144 plus an offset of at most 32768 either way (owner 0 at 0), and some owner in every row has exactly 327680.
All inputs are finite; a program needn't handle non-finite values.
Results may differ from the reference program's by a relative error of at most 0.022.
Values may be sent and summed in bfloat16 or wider, within the bound.
A program may use at most 128 MiB of HBM per device.

```python
import math
import jax
import jax.numpy as jnp
from jax import lax

D = 8192
KVW = 512
MB = 4
TOK_MB = 32
SECTIONS = 8
REPLICAS = 16
COLS = 256
ROWS = 512
PARAMS = 4194304
OWN_MAX = 327680
N_SECTION = 8
N_DP = 16
N_TENSOR = 2


def draw_owner_lengths(key, part):
    key = jax.random.fold_in(key, 7)
    even_size = PARAMS // REPLICAS
    reach = even_size // 8
    key_moves, key_pick = jax.random.split(key)
    moves = jax.random.randint(key_moves, (SECTIONS, N_TENSOR, REPLICAS - 1), -reach, reach + 1, dtype=jnp.int32)
    picked = jax.random.randint(key_pick, (SECTIONS, N_TENSOR, 1), 1, REPLICAS - 1, dtype=jnp.int32)
    bound_index = jnp.arange(REPLICAS - 1, dtype=jnp.int32)[None, None, :]
    moves = jnp.where(bound_index == picked - 1, -reach, moves)
    moves = jnp.where(bound_index == picked, reach, moves)
    bounds = (bound_index + 1) * even_size + moves
    first_edge = jnp.zeros((SECTIONS, N_TENSOR, 1), jnp.int32)
    last_edge = jnp.full((SECTIONS, N_TENSOR, 1), PARAMS, jnp.int32)
    edges = jnp.concatenate([first_edge, bounds, last_edge], axis=2)
    return (edges[:, :, 1:] - edges[:, :, :-1]).astype(jnp.int32)


def levels(key, extent, pieces, least, largest):
    factor_of = 1.0
    for dim, blocks in pieces:
        heights = jax.random.uniform(jax.random.fold_in(jax.random.fold_in(key, 6), dim), (blocks,), jnp.float32, least / len(pieces), largest / len(pieces))
        factor_of = factor_of * jnp.repeat(jnp.exp(heights), extent[dim] // blocks).reshape((-1,) + (1,) * (len(extent) - 1 - dim))
    return factor_of


def noise(rng, dims, spread, most, pieces=(), kind=jnp.bfloat16):
    array = spread * jax.random.normal(rng, dims, jnp.float32)
    if pieces:
        array = array * levels(rng, dims, pieces, -0.22, 0.18)
    return jnp.clip(array, -most, most).astype(kind)


def setup_inputs(seed: int = 0) -> dict:
    key_list = jax.random.split(jax.random.key(seed), 9)
    section_inputs = noise(key_list[0], (SECTIONS, MB, ROWS, D), 1.0, 6.0, ((0, 8), (2, 32)))
    top_grad = noise(key_list[1], (MB, ROWS, D), 1.0, 6.0, ((1, 32),))
    value_weight = noise(key_list[2], (SECTIONS, D, KVW), D ** -0.5, 0.0625, ((0, 8), (1, 16), (2, 2)))
    output_weight = noise(key_list[3], (SECTIONS, KVW, D), D ** -0.5, 0.0625, ((0, 8), (1, 2), (2, 16)))
    owner_lengths = draw_owner_lengths(jax.random.fold_in(key_list[8], 71), 0)
    master_param = noise(key_list[5], (SECTIONS, N_TENSOR, REPLICAS * OWN_MAX), 1.0, 6.0, ((0, 8), (1, 2), (2, 16)), jnp.float32)
    moment1 = noise(key_list[6], (SECTIONS, N_TENSOR, REPLICAS * OWN_MAX), 0.3, 4.0, ((0, 8), (1, 2), (2, 16)), jnp.float32)
    moment2 = jnp.clip(jnp.exp(math.log(2.0) - 3.6888794 * jax.random.uniform(key_list[7], (SECTIONS, N_TENSOR, REPLICAS * OWN_MAX), jnp.float32) ** levels(key_list[7], (SECTIONS, N_TENSOR, REPLICAS * OWN_MAX), ((0, 8), (1, 2), (2, 16)), -0.2, 0.2)), 0.05, 2.0)
    return {"section_inputs": section_inputs, "top_grad": top_grad, "value_weight": value_weight, "output_weight": output_weight, "owner_lengths": owner_lengths, "master_param": master_param, "moment1": moment1, "moment2": moment2}


beta_one = 0.9
beta_two = 0.95
learn_rate = 0.001
decay_rate = 0.1
adam_eps = 1e-08
adam_step = 20.0

def adam_update(master_value, first_moment, second_moment, grad_value):
    first_new = beta_one * first_moment + (1.0 - beta_one) * grad_value
    second_new = beta_two * second_moment + (1.0 - beta_two) * grad_value * grad_value
    corrected = first_new / (1.0 - beta_one ** adam_step) / (jnp.sqrt(second_new / (1.0 - beta_two ** adam_step)) + adam_eps)
    return (master_value - learn_rate * (corrected + decay_rate * master_value), first_new, second_new)

def owner_pieces(flat_grad, lengths, own_max):
    starts = jnp.cumsum(lengths, dtype=jnp.int32) - lengths
    offsets = jnp.arange(own_max, dtype=jnp.int32)
    positions = jnp.clip(starts[:, None] + offsets[None, :], 0, flat_grad.shape[0] - 1)
    return jnp.where(offsets[None, :] < lengths[:, None], flat_grad[positions], jnp.zeros((), flat_grad.dtype))

def by_replica(block, columns):
    return block.reshape(MB, N_DP, TOK_MB, columns).transpose(1, 0, 2, 3).reshape(N_DP, MB * TOK_MB, columns)

def reference(section_inputs, top_grad, value_weight, output_weight, owner_lengths, master_param, moment1, moment2):
    grad_scale = 1.0 / math.sqrt(MB * TOK_MB * N_DP)
    incoming = top_grad.reshape(MB * ROWS, D)
    grads_list = [None] * N_SECTION
    param_list = [[None] * N_TENSOR for section_index in range(N_SECTION)]
    first_list = [[None] * N_TENSOR for section_index in range(N_SECTION)]
    second_list = [[None] * N_TENSOR for section_index in range(N_SECTION)]

    def add_replica(totals, loop_item):
        rows_in, rows_vgrad, rows_value, rows_grad = loop_item
        value_part = jnp.dot(rows_in.T, rows_vgrad, preferred_element_type=jnp.float32) * grad_scale
        output_part = jnp.dot(rows_value.T, rows_grad, preferred_element_type=jnp.float32) * grad_scale
        grad_piece = lax.optimization_barrier(jnp.concatenate([value_part.astype(jnp.bfloat16).reshape(-1), output_part.astype(jnp.bfloat16).reshape(-1)]))
        return (totals + grad_piece.astype(jnp.float32), None)
    for section_index in range(N_SECTION - 1, -1, -1):
        inputs = section_inputs[section_index].reshape(MB * ROWS, D)
        summed_rows = incoming.astype(jnp.float32)
        for part_index in range(N_TENSOR):
            col_start = part_index * COLS
            value_cols = value_weight[section_index, :, col_start:col_start + COLS]
            output_part_rows = output_weight[section_index, col_start:col_start + COLS, :]
            value_grad = jnp.dot(incoming, output_part_rows.T, preferred_element_type=jnp.float32).astype(jnp.bfloat16)
            branch = lax.optimization_barrier(jnp.dot(value_grad, value_cols.T, preferred_element_type=jnp.float32).astype(jnp.bfloat16))
            summed_rows = summed_rows + branch.astype(jnp.float32)
            values = jnp.dot(inputs, value_cols, preferred_element_type=jnp.float32).astype(jnp.bfloat16)
            flat_grad, unused = lax.scan(add_replica, jnp.zeros((PARAMS,), jnp.float32), (by_replica(inputs, D), by_replica(value_grad, COLS), by_replica(values, COLS), by_replica(incoming, D)))
            owner_grad = owner_pieces(flat_grad, owner_lengths[section_index, part_index], OWN_MAX).reshape(-1)
            updated = adam_update(master_param[section_index, part_index], moment1[section_index, part_index], moment2[section_index, part_index], owner_grad)
            param_list[section_index][part_index] = updated[0]
            first_list[section_index][part_index] = updated[1]
            second_list[section_index][part_index] = updated[2]
        incoming = summed_rows.astype(jnp.bfloat16)
        grads_list[section_index] = incoming.reshape(MB, ROWS, D)
    input_grads = jnp.stack(grads_list)
    new_param = jnp.stack([jnp.stack(row_list) for row_list in param_list])
    new_moment1 = jnp.stack([jnp.stack(row_list) for row_list in first_list])
    new_moment2 = jnp.stack([jnp.stack(row_list) for row_list in second_list])
    return (input_grads, new_param, new_moment1, new_moment2)
```

```python
import functools
import math

import jax
import jax.numpy as jnp
from jax import lax
from jax.experimental import pallas as pl
from jax.experimental.pallas import tpu as pltpu
from jax.sharding import PartitionSpec as P

MESH = pl.DeviceIdType.MESH
BF16 = jnp.bfloat16
F32 = jnp.float32

beta_one = 0.9
beta_two = 0.95
learn_rate = 0.001
decay_rate = 0.1
adam_eps = 1e-08
adam_step = 20.0

CHUNKS = 8
NT = (((1,), (1,)), ((), ()))
NN = (((1,), (0,)), ((), ()))
TN = (((0,), (0,)), ((), ()))


def dot(a, b, dims):
    return lax.dot_general(a, b, dims, preferred_element_type=F32)


def device(x, y, z, t):
    return (2 * x + lax.div(z, 4), lax.rem(z, 4) * 4 + y, t)


def aligned(start, size):
    return pl.ds(pl.multiple_of(start, size), size)


def wait_bytes(ref, sem):
    pltpu.make_async_copy(ref, ref, sem).wait()


def relay_kernel(
    xin, top, vw, ow,
    out, vwin, owin,
    gin, gout, xrow, vst, ost, vd, od, pbuf, rsb, vg, gd, pv, rsv, val, xd, accv, acco, dvb, dob,
    s_x, s_w1, s_w2, s_top, s_rs, s_ag, s_hop, s_out, s_gd, s_vg, s_rsv, s_agv, s_val, s_xd, s_own,
    r_x, r_w1, r_w2, r_g, r_rs, r_ag, r_gd, r_vg, r_rsv, r_agv, r_val, r_xd, r_own, r_out,
):
    sec = lax.axis_index("section")
    dp = lax.axis_index("dp")
    t = lax.axis_index("tensor")
    x = lax.div(sec, 2)
    zl = lax.div(dp, 4)
    y = lax.rem(dp, 4)
    z = lax.rem(sec, 2) * 4 + zl

    def is_me(to):
        return jnp.logical_and(jnp.logical_and(to[0] == sec, to[1] == dp), to[2] == t)

    def send(src, dst, ssem, rsem, to):
        mine = is_me(to)

        @pl.when(mine)
        def _():
            pltpu.make_async_copy(src, dst, rsem).start()

        @pl.when(jnp.logical_not(mine))
        def _():
            pltpu.make_async_remote_copy(src, dst, ssem, rsem, device_id=to, device_id_type=MESH).start()

    def sent(src, ssem, to):
        @pl.when(jnp.logical_not(is_me(to)))
        def _():
            wait_bytes(src, ssem)

    def push(src, dst, ssem, rsem, to):
        pltpu.make_async_remote_copy(src, dst, ssem, rsem, device_id=to, device_id_type=MESH).start()

    w1_to = device(zl, y, sec, t)
    send(vw, vst, s_w1.at[0], r_w1.at[0], w1_to)
    send(ow, ost, s_w1.at[1], r_w1.at[1], w1_to)

    half = lax.div(zl, 2)
    row16 = aligned(lax.rem(zl, 2) * 32 + t * 16, 16)
    top_sender = jnp.logical_or(z < 2, z >= 6)

    def top_parts():
        for mb in range(4):
            for t2 in range(2):
                src = top.at[mb, :, aligned(x * 2048 + t2 * 1024, 1024)]
                yield mb * 2 + t2, src, mb * 2 + half, device(x, y, 7, t2)

    @pl.when(top_sender)
    def _():
        for k, src, c, to in top_parts():
            send(src, gin.at[c, row16, :], s_top.at[k], r_g.at[c], to)

    def x_parts():
        for x2 in range(4):
            for t2 in range(2):
                src = xin.at[:, :, pl.ds(x2 * 2048 + t2 * 1024, 1024)]
                yield x2 * 2 + t2, src, device(x2, y, sec, t2)

    for k, src, to in x_parts():
        send(src, xrow.at[:, half, row16, :], s_x.at[k], r_x, to)

    wait_bytes(vst, r_w1.at[0])
    wait_bytes(ost, r_w1.at[1])

    def w2_parts():
        rows = aligned(lax.rem(y, 2) * 512, 512)
        cols = aligned(t * 256, 256)
        for y2 in range(4):
            to = device(x, y2, z, lax.div(y, 2))
            yield y2, vst, vd.at[rows, cols], 0, to
            yield 4 + y2, ost, od.at[cols, rows], 1, to

    for k, src, dst, r, to in w2_parts():
        send(src, dst, s_w2.at[k], r_w2.at[r], to)
    wait_bytes(vd, r_w2.at[0])
    wait_bytes(od, r_w2.at[1])

    def peers():
        for k in range(1, 8):
            yield k - 1, lax.rem(x + k // 2, 4), lax.rem(t + k % 2, 2)

    def y_peers():
        for k in range(1, 4):
            yield k - 1, lax.rem(y + k, 4)

    def xd_parts():
        for y2 in range(4):
            yield y2, xrow.at[:, :, :, pl.ds(y2 * 256, 256)], device(x, y2, z, t)

    def values_stage():
        wait_bytes(xrow, r_x)
        for k, src, to in xd_parts():
            send(src, xd.at[y], s_xd.at[k], r_xd, to)

        def block(i, carry):
            rows = xrow[lax.div(i, 2), lax.rem(i, 2)]
            pv[aligned(i * 64, 64), :] = dot(rows, vd[...], NN).astype(BF16)
            return carry

        lax.fori_loop(0, 8, block, 0)
        for k, x2, t2 in peers():
            push(
                pv.at[aligned(x2 * 128, 128), aligned(t2 * 256, 256)], rsv.at[k], s_rsv, r_rsv, device(x2, y, z, t2)
            )
        wait_bytes(rsv, r_rsv)
        rows, cols = aligned(x * 128, 128), aligned(t * 256, 256)
        total = pv[rows, cols].astype(F32)
        for k in range(7):
            total = total + rsv[k].astype(F32)
        val[y, rows, cols] = total.astype(BF16)
        mine = val.at[y, rows, cols]
        for k, x2, t2 in peers():
            push(mine, mine, s_agv, r_agv, device(x2, y, z, t2))
        wait_bytes(rsv, r_agv)
        for k, y2 in y_peers():
            push(val.at[y], val.at[y], s_val.at[k], r_val, device(x, y2, z, t))

    @pl.when(z < 4)
    def _():
        values_stage()

    def gd_parts(c):
        for y2 in range(4):
            yield y2, gin.at[c, :, pl.ds(y2 * 256, 256)], device(x, y2, z, t)

    def out_parts(c):
        for a in range(2):
            for t2 in range(2):
                to = (z, (2 * lax.rem(c, 2) + a) * 4 + y, t2)
                yield a * 2 + t2, gout.at[c, pl.ds(a * 32 + t2 * 16, 16), :], to

    def relay_step(c, carry):
        wait_bytes(gin.at[c], r_g.at[c])
        pbuf[c] = dot(gin[c], od[...], NT).astype(BF16)
        for k, x2, t2 in peers():
            push(
                pbuf.at[c, aligned(x2 * 16, 16), aligned(t2 * 256, 256)],
                rsb.at[c, k],
                s_rs.at[c],
                r_rs.at[c],
                device(x2, y, z, t2),
            )
        for k, src, to in gd_parts(c):
            send(src, gd.at[y, c], s_gd.at[c, k], r_gd, to)
        wait_bytes(rsb.at[c], r_rs.at[c])
        rows, cols = aligned(x * 16, 16), aligned(t * 256, 256)
        total = pbuf[c, rows, cols].astype(F32)
        for k in range(7):
            total = total + rsb[c, k].astype(F32)
        vg[y, c, rows, cols] = total.astype(BF16)
        mine = vg.at[y, c, rows, cols]
        for k, x2, t2 in peers():
            push(mine, mine, s_ag.at[c], r_ag.at[c], device(x2, y, z, t2))
        wait_bytes(rsb.at[c], r_ag.at[c])
        branch = dot(vg[y, c], vd[...], NT)
        gout[c] = (gin[c].astype(F32) + branch).astype(BF16)

        @pl.when(z > 0)
        def _():
            push(gout.at[c], gin.at[c], s_hop.at[c], r_g.at[c], device(x, y, z - 1, t))

        for k, src, to in out_parts(c):
            send(src, out.at[lax.div(c, 2), :, aligned(x * 2048 + t * 1024, 1024)], s_out.at[c, k], r_out, to)
        for k, y2 in y_peers():
            push(vg.at[y, c], vg.at[y, c], s_vg.at[c, k], r_vg, device(x, y2, z, t))
        return carry

    lax.fori_loop(0, CHUNKS, relay_step, 0)

    @pl.when(z >= 4)
    def _():
        values_stage()

    wait_bytes(xd, r_xd)
    wait_bytes(val.at[pl.ds(0, 3)], r_val)
    wait_bytes(gd, r_gd)
    wait_bytes(vg.at[pl.ds(0, 3)], r_vg)
    accv[...] = jnp.zeros_like(accv)
    acco[...] = jnp.zeros_like(acco)

    def grad_step(j, carry):
        accv[...] += dot(xd[j].reshape(512, 256), vg[j].reshape(512, 512), TN)
        acco[...] += dot(val[j], gd[j].reshape(512, 256), TN)
        return carry

    lax.fori_loop(0, 4, grad_step, 0)
    scale = 1.0 / math.sqrt(2048)
    for t2 in range(2):
        dvb[t2] = (accv[:, t2 * 256 : t2 * 256 + 256] * scale).astype(BF16)
        dob[t2, 0:16, :] = jnp.zeros((16, 256), BF16)
        dob[t2, 16:272, :] = (acco[t2 * 256 : t2 * 256 + 256, :] * scale).astype(BF16)
        dob[t2, 272:288, :] = jnp.zeros((16, 256), BF16)

    owner = 2 * x + t
    place = 8 * x + 4 * t + y

    def owner_parts(t2):
        yield 0, dvb.at[t2], vwin.at[pl.ds(pl.multiple_of(128 + y * 256, 128), 256)], 0, (z, owner, t2), None
        yield 1, dvb.at[t2, pl.ds(128, 128)], vwin.at[pl.ds(0, 128)], 1, (z, owner + 1, t2), y == 3
        yield 2, dvb.at[t2, pl.ds(0, 128)], vwin.at[pl.ds(1152, 128)], 2, (z, owner - 1, t2), jnp.logical_and(
            y == 0, owner >= 1
        )
        for k in range(8):
            yield 3 + k, dob.at[t2, pl.ds(32 * k, 64)], owin.at[place], 3, (z, 8 + k, t2), None
        yield 11, dob.at[t2, pl.ds(16, 16)], owin.at[place, pl.ds(48, 16)], 3, (z, 7, t2), None

    def guarded(cond, what):
        if cond is None:
            what()
        else:
            pl.when(cond)(what)

    for t2 in range(2):
        for k, src, dst, r, to, cond in owner_parts(t2):
            guarded(cond, functools.partial(send, src, dst, s_own.at[t2, k], r_own.at[r], to))

    @pl.when(dp <= 7)
    def _():
        wait_bytes(vwin.at[pl.ds(128, 1024)], r_own.at[0])

    @pl.when(jnp.logical_and(dp >= 1, dp <= 8))
    def _():
        wait_bytes(vwin.at[pl.ds(0, 128)], r_own.at[1])

    @pl.when(dp <= 6)
    def _():
        wait_bytes(vwin.at[pl.ds(1152, 128)], r_own.at[2])

    @pl.when(dp == 7)
    def _():
        wait_bytes(owin.at[pl.ds(0, 8)], r_own.at[3])

    @pl.when(dp >= 8)
    def _():
        wait_bytes(owin, r_own.at[3])

    wait_bytes(out, r_out)

    sent(vw, s_w1.at[0], w1_to)
    sent(ow, s_w1.at[1], w1_to)

    @pl.when(top_sender)
    def _():
        for k, src, c, to in top_parts():
            sent(src, s_top.at[k], to)

    for k, src, to in x_parts():
        sent(src, s_x.at[k], to)
    for k, src, dst, r, to in w2_parts():
        sent(src, s_w2.at[k], to)
    for k, src, to in xd_parts():
        sent(src, s_xd.at[k], to)
    wait_bytes(rsv, s_rsv)
    wait_bytes(rsv, s_agv)
    for k, y2 in y_peers():
        wait_bytes(val.at[y], s_val.at[k])

    def drain(c, carry):
        wait_bytes(rsb.at[c], s_rs.at[c])
        wait_bytes(rsb.at[c], s_ag.at[c])
        for k, src, to in gd_parts(c):
            sent(src, s_gd.at[c, k], to)

        @pl.when(z > 0)
        def _():
            wait_bytes(gout.at[c], s_hop.at[c])

        for k, src, to in out_parts(c):
            sent(src, s_out.at[c, k], to)
        for k, y2 in y_peers():
            wait_bytes(vg.at[y, c], s_vg.at[c, k])
        return carry

    lax.fori_loop(0, CHUNKS, drain, 0)
    for t2 in range(2):
        for k, src, dst, r, to, cond in owner_parts(t2):
            guarded(cond, functools.partial(sent, src, s_own.at[t2, k], to))


def relay(xin, top, vw, ow):
    hbm = pl.BlockSpec(memory_space=pl.ANY)
    dma = pltpu.SemaphoreType.DMA
    return pl.pallas_call(
        relay_kernel,
        out_shape=(
            jax.ShapeDtypeStruct((4, 16, 8192), BF16),
            jax.ShapeDtypeStruct((1280, 256), BF16),
            jax.ShapeDtypeStruct((32, 64, 256), BF16),
        ),
        in_specs=[hbm] * 4,
        out_specs=(hbm, hbm, hbm),
        scratch_shapes=[
            pltpu.VMEM((CHUNKS, 64, 1024), BF16),
            pltpu.VMEM((CHUNKS, 64, 1024), BF16),
            pltpu.VMEM((4, 2, 64, 1024), BF16),
            pltpu.VMEM((512, 256), BF16),
            pltpu.VMEM((256, 512), BF16),
            pltpu.VMEM((1024, 512), BF16),
            pltpu.VMEM((512, 1024), BF16),
            pltpu.VMEM((CHUNKS, 64, 512), BF16),
            pltpu.VMEM((CHUNKS, 7, 16, 256), BF16),
            pltpu.VMEM((4, CHUNKS, 64, 512), BF16),
            pltpu.VMEM((4, CHUNKS, 64, 256), BF16),
            pltpu.VMEM((512, 512), BF16),
            pltpu.VMEM((7, 128, 256), BF16),
            pltpu.VMEM((4, 512, 512), BF16),
            pltpu.VMEM((4, 4, 2, 64, 256), BF16),
            pltpu.VMEM((256, 512), F32),
            pltpu.VMEM((512, 256), F32),
            pltpu.VMEM((2, 256, 256), BF16),
            pltpu.VMEM((2, 288, 256), BF16),
            dma((8,)), dma((2,)), dma((8,)), dma((8,)),
            dma((CHUNKS,)), dma((CHUNKS,)), dma((CHUNKS,)), dma((CHUNKS, 4)),
            dma((CHUNKS, 4)), dma((CHUNKS, 3)), dma, dma,
            dma((3,)), dma((4,)), dma((2, 12)),
            dma, dma((2,)), dma((2,)), dma((CHUNKS,)),
            dma((CHUNKS,)), dma((CHUNKS,)), dma, dma, dma, dma,
            dma, dma, dma((4,)), dma,
        ],
        compiler_params=pltpu.CompilerParams(has_side_effects=True, vmem_limit_bytes=48 * 1024 * 1024),
    )(xin, top, vw, ow)


def adam_kernel(steps, lengths, vwin, owin, param, first, second, new_param, new_first, new_second, flat):
    dp = lax.axis_index("dp")
    step = pl.program_id(0)
    rows = param.shape[0]

    def from_value(low, high):
        for a in range(low, high, 128):
            part = vwin[a : a + 128, :].astype(F32)
            flat[pl.ds(2 * a, 128, stride=2), :] = part[:, :128]
            flat[pl.ds(2 * a + 1, 128, stride=2), :] = part[:, 128:]

    def from_output(low, high):
        for e in range(32):
            part = owin[e].astype(F32)[12 + low : 12 + high, :]
            for h in range(2):
                flat[pl.ds(low * 64 + e * 2 + h, high - low, stride=64), :] = part[:, h * 128 : h * 128 + 128]

    @pl.when(step == 0)
    def _():
        flat[2560:, :] = jnp.zeros((flat.shape[0] - 2560, 128), F32)
        for last, value_rows, output_rows in ((8, (0, 128), (0, 4)), (7, (128, 1152), (4, 36)), (6, (1152, 1280), (36, 40))):
            pl.when(dp <= last)(functools.partial(from_value, *value_rows))
            pl.when(dp > last)(functools.partial(from_output, *output_rows))

    start = lax.fori_loop(0, dp, lambda e, total: total + lengths[e], jnp.int32(0))
    length = lengths[dp]
    offset = start - dp * 262144 + 32768
    row, lane = lax.div(offset, 128), lax.rem(offset, 128)
    window = flat[pl.ds(step * rows + row, rows + 8), :]
    turned = pltpu.roll(window, lax.rem(128 - lane, 128), 1)
    lanes = lax.broadcasted_iota(jnp.int32, (rows, 128), 1)
    grad = jnp.where(lanes < 128 - lane, turned[:rows], turned[1 : rows + 1])
    index = (step * rows + lax.broadcasted_iota(jnp.int32, (rows, 128), 0)) * 128 + lanes
    grad = jnp.where(index < length, grad, 0.0)

    first_new = beta_one * first[...] + (1.0 - beta_one) * grad
    second_new = beta_two * second[...] + (1.0 - beta_two) * grad * grad
    corrected = (
        first_new
        / (1.0 - beta_one**adam_step)
        / (jnp.sqrt(second_new / (1.0 - beta_two**adam_step)) + adam_eps)
    )
    new_param[...] = param[...] - learn_rate * (corrected + decay_rate * param[...])
    new_first[...] = first_new
    new_second[...] = second_new


def adam(lengths, vwin, owin, param, first, second):
    steps = 5
    block = pl.BlockSpec((2560 // steps, 128), lambda i: (i, 0))
    shape = jax.ShapeDtypeStruct((2560, 128), F32)
    return pl.pallas_call(
        functools.partial(adam_kernel, steps),
        grid=(steps,),
        out_shape=(shape, shape, shape),
        in_specs=[
            pl.BlockSpec(memory_space=pltpu.SMEM),
            pl.BlockSpec(memory_space=pltpu.VMEM),
            pl.BlockSpec(memory_space=pltpu.VMEM),
            block,
            block,
            block,
        ],
        out_specs=(block, block, block),
        scratch_shapes=[pltpu.VMEM((2560 + 528, 128), F32)],
        compiler_params=pltpu.CompilerParams(vmem_limit_bytes=32 * 1024 * 1024),
    )(lengths, vwin, owin, param, first, second)


def local(section_inputs, top_grad, value_weight, output_weight, owner_lengths, master_param, moment1, moment2):
    out, vwin, owin = relay(section_inputs[0], top_grad, value_weight[0], output_weight[0])
    flat = (2560, 128)
    updated = adam(
        owner_lengths[0, 0], vwin, owin, master_param.reshape(flat), moment1.reshape(flat), moment2.reshape(flat)
    )
    return (out[None], *(array.reshape(1, 1, -1) for array in updated))


def solution(mesh):
    in_specs = (
        P("section", None, ("dp", "tensor"), None),
        P(None, ("dp", "tensor"), None),
        P("section", "dp", "tensor"),
        P("section", "tensor", "dp"),
        P("section", "tensor", None),
        P("section", "tensor", "dp"),
        P("section", "tensor", "dp"),
        P("section", "tensor", "dp"),
    )
    out_specs = (
        P("section", None, ("dp", "tensor"), None),
        P("section", "tensor", "dp"),
        P("section", "tensor", "dp"),
        P("section", "tensor", "dp"),
    )
    return jax.shard_map(local, mesh=mesh, in_specs=in_specs, out_specs=out_specs, check_vma=False)
```

```python
import functools
import math

import jax
import jax.numpy as jnp
from jax import lax
from jax.experimental import pallas as pl
from jax.experimental.pallas import tpu as pltpu
from jax.sharding import PartitionSpec as P

MESH = pl.DeviceIdType.MESH
BF16 = jnp.bfloat16
F32 = jnp.float32

beta_one = 0.9
beta_two = 0.95
learn_rate = 0.001
decay_rate = 0.1
adam_eps = 1e-08
adam_step = 20.0

CHUNKS = 8
NT = (((1,), (1,)), ((), ()))
NN = (((1,), (0,)), ((), ()))
TN = (((0,), (0,)), ((), ()))


def dot(a, b, dims):
    return lax.dot_general(a, b, dims, preferred_element_type=F32)


def device(x, y, z, t):
    return (2 * x + lax.div(z, 4), lax.rem(z, 4) * 4 + y, t)


def aligned(start, size):
    return pl.ds(pl.multiple_of(start, size), size)


def wait_bytes(ref, sem):
    pltpu.make_async_copy(ref, ref, sem).wait()


def relay_kernel(
    xin, top, vw, ow,
    out, vwin, owin,
    gin, gout, xrow, xst, vwst, owst, vst, ost, vd, od, pbuf, rsb, vg, gd, pv, rsv, val, xd, accv, acco, dvb, dob,
    s_xa, s_x, s_wa, s_w1, s_w2, s_top, s_rs, s_ag, s_hop, s_out, s_gd, s_vg, s_rsv, s_agv, s_val, s_xd, s_own,
    r_xa, r_x, r_wa, r_w1, r_w2, r_g, r_rs, r_ag, r_gd, r_vg, r_rsv, r_agv, r_val, r_xd, r_own, r_out,
):
    sec = lax.axis_index("section")
    dp = lax.axis_index("dp")
    t = lax.axis_index("tensor")
    x = lax.div(sec, 2)
    zl = lax.div(dp, 4)
    y = lax.rem(dp, 4)
    z = lax.rem(sec, 2) * 4 + zl

    def is_me(to):
        return jnp.logical_and(jnp.logical_and(to[0] == sec, to[1] == dp), to[2] == t)

    def send(src, dst, ssem, rsem, to):
        mine = is_me(to)

        @pl.when(mine)
        def _():
            pltpu.make_async_copy(src, dst, rsem).start()

        @pl.when(jnp.logical_not(mine))
        def _():
            pltpu.make_async_remote_copy(src, dst, ssem, rsem, device_id=to, device_id_type=MESH).start()

    def sent(src, ssem, to):
        @pl.when(jnp.logical_not(is_me(to)))
        def _():
            wait_bytes(src, ssem)

    def push(src, dst, ssem, rsem, to):
        pltpu.make_async_remote_copy(src, dst, ssem, rsem, device_id=to, device_id_type=MESH).start()

    zh = lax.rem(sec, 2)
    wa_to = device(zl, y, z, t)
    send(vw, vwst.at[x], s_wa.at[0], r_wa.at[x, 0], wa_to)
    send(ow, owst.at[x], s_wa.at[1], r_wa.at[x, 1], wa_to)

    half = lax.div(zl, 2)
    row16 = aligned(lax.rem(zl, 2) * 32 + t * 16, 16)
    top_sender = jnp.logical_or(z < 2, z >= 6)

    def top_parts():
        for mb in range(4):
            for t2 in range(2):
                src = top.at[mb, :, aligned(x * 2048 + t2 * 1024, 1024)]
                yield mb * 2 + t2, src, mb * 2 + half, device(x, y, 7, t2)

    @pl.when(top_sender)
    def _():
        for k, src, c, to in top_parts():
            send(src, gin.at[c, row16, :], s_top.at[k], r_g.at[c], to)

    def x_parts():
        for x2 in range(4 ):
            for t2 in range(2):
                yield x2 * 2 + t2, xin.at[:, :, pl.ds(x2 * 2048 + t2 * 1024, 1024)], device(x2, y, z, t2)

    def x_moves():
        for x2 in reversed(range(4 )):
            yield x2, xst.at[x2], device(x, y, 2 * x2 + zh, t)

    @pl.when(x == zl)
    def _():
        for x2 in reversed(range(4)):
            to = device(x, y, 2 * x2 + zh, t)
            wait_bytes(vwst.at[x2], r_wa.at[x2, 0])
            send(vwst.at[x2], vst, s_w1.at[x2, 0], r_w1.at[0], to)
            wait_bytes(owst.at[x2], r_wa.at[x2, 1])
            send(owst.at[x2], ost, s_w1.at[x2, 1], r_w1.at[1], to)

    wait_bytes(vst, r_w1.at[0])
    wait_bytes(ost, r_w1.at[1])
    for k, src, to in x_parts():
        send(src, xst.at[x, :, aligned(t * 16, 16), :], s_xa.at[k], r_xa.at[x], to)

    def w2_parts():
        rows = aligned(lax.rem(y, 2) * 512, 512)
        cols = aligned(t * 256, 256)
        for y2 in range(4):
            to = device(x, y2, z, lax.div(y, 2))
            yield y2, vst, vd.at[rows, cols], 0, to
            yield 4 + y2, ost, od.at[cols, rows], 1, to

    for k, src, dst, r, to in w2_parts():
        send(src, dst, s_w2.at[k], r_w2.at[r], to)
    wait_bytes(vd, r_w2.at[0])
    wait_bytes(od, r_w2.at[1])
    for k, src, to in x_moves():
        wait_bytes(src, r_xa.at[k])
        send(src, xrow.at[:, half, aligned(lax.rem(zl, 2) * 32, 32), :], s_x.at[k], r_x, to)

    def peers():
        for k in range(1, 8):
            yield k - 1, lax.rem(x + k // 2, 4), lax.rem(t + k % 2, 2)

    def y_peers():
        for k in range(1, 4):
            yield k - 1, lax.rem(y + k, 4)

    def xd_parts():
        for y2 in range(4):
            yield y2, xrow.at[:, :, :, pl.ds(y2 * 256, 256)], device(x, y2, z, t)

    def values_stage():
        wait_bytes(xrow, r_x)
        for k, src, to in xd_parts():
            send(src, xd.at[y], s_xd.at[k], r_xd, to)

        def block(i, carry):
            rows = xrow[lax.div(i, 2), lax.rem(i, 2)]
            pv[aligned(i * 64, 64), :] = dot(rows, vd[...], NN).astype(BF16)
            return carry

        lax.fori_loop(0, 8, block, 0)
        for k, x2, t2 in peers():
            push(
                pv.at[aligned(x2 * 128, 128), aligned(t2 * 256, 256)], rsv.at[k], s_rsv, r_rsv, device(x2, y, z, t2)
            )
        wait_bytes(rsv, r_rsv)
        rows, cols = aligned(x * 128, 128), aligned(t * 256, 256)
        total = pv[rows, cols].astype(F32)
        for k in range(7):
            total = total + rsv[k].astype(F32)
        val[y, rows, cols] = total.astype(BF16)
        mine = val.at[y, rows, cols]
        for k, x2, t2 in peers():
            push(mine, mine, s_agv, r_agv, device(x2, y, z, t2))
        wait_bytes(rsv, r_agv)
        for k, y2 in y_peers():
            push(val.at[y], val.at[y], s_val.at[k], r_val, device(x, y2, z, t))

    @pl.when(z < 3)
    def _():
        values_stage()

    def gd_parts(c):
        for y2 in range(4):
            yield y2, gin.at[c, :, pl.ds(y2 * 256, 256)], device(x, y2, z, t)

    def out_parts(c):
        for a in range(2):
            for t2 in range(2):
                to = (z, (2 * lax.rem(c, 2) + a) * 4 + y, t2)
                yield a * 2 + t2, gout.at[c, pl.ds(a * 32 + t2 * 16, 16), :], to

    def first_part(c):
        wait_bytes(gin.at[c], r_g.at[c])
        pbuf[c] = dot(gin[c], od[...], NT).astype(BF16)
        for k, x2, t2 in peers():
            push(
                pbuf.at[c, aligned(x2 * 16, 16), aligned(t2 * 256, 256)],
                rsb.at[c, k],
                s_rs.at[c],
                r_rs.at[c],
                device(x2, y, z, t2),
            )
        for k, src, to in gd_parts(c):
            send(src, gd.at[y, c], s_gd.at[c, k], r_gd, to)

    def second_part(c):
        wait_bytes(rsb.at[c], r_rs.at[c])
        rows, cols = aligned(x * 16, 16), aligned(t * 256, 256)
        total = pbuf[c, rows, cols].astype(F32)
        for k in range(7):
            total = total + rsb[c, k].astype(F32)
        vg[y, c, rows, cols] = total.astype(BF16)
        mine = vg.at[y, c, rows, cols]
        for k, x2, t2 in peers():
            push(mine, mine, s_ag.at[c], r_ag.at[c], device(x2, y, z, t2))

    def third_part(c):
        wait_bytes(rsb.at[c], r_ag.at[c])
        branch = dot(vg[y, c], vd[...], NT)
        gout[c] = (gin[c].astype(F32) + branch).astype(BF16)

        @pl.when(z > 0)
        def _():
            push(gout.at[c], gin.at[c], s_hop.at[c], r_g.at[c], device(x, y, z - 1, t))

        for k, src, to in out_parts(c):
            send(src, out.at[lax.div(c, 2), :, aligned(x * 2048 + t * 1024, 1024)], s_out.at[c, k], r_out, to)
        for k, y2 in y_peers():
            push(vg.at[y, c], vg.at[y, c], s_vg.at[c, k], r_vg, device(x, y2, z, t))

    def relay_step(c, carry):
        second_part(c)

        @pl.when(c + 1 < CHUNKS)
        def _():
            first_part(c + 1)

        third_part(c)
        return carry

    first_part(0)
    lax.fori_loop(0, CHUNKS, relay_step, 0)

    @pl.when(z >= 3)
    def _():
        values_stage()

    wait_bytes(xd, r_xd)
    wait_bytes(val.at[pl.ds(0, 3)], r_val)
    wait_bytes(gd, r_gd)
    wait_bytes(vg.at[pl.ds(0, 3)], r_vg)
    accv[...] = jnp.zeros_like(accv)
    acco[...] = jnp.zeros_like(acco)

    def grad_step(j, carry):
        accv[...] += dot(xd[j].reshape(512, 256), vg[j].reshape(512, 512), TN)
        acco[...] += dot(val[j], gd[j].reshape(512, 256), TN)
        return carry

    lax.fori_loop(0, 4, grad_step, 0)
    scale = 1.0 / math.sqrt(2048)
    for t2 in range(2):
        dvb[t2] = (accv[:, t2 * 256 : t2 * 256 + 256] * scale).astype(BF16)
        dob[t2, 0:16, :] = jnp.zeros((16, 256), BF16)
        dob[t2, 16:272, :] = (acco[t2 * 256 : t2 * 256 + 256, :] * scale).astype(BF16)
        dob[t2, 272:288, :] = jnp.zeros((16, 256), BF16)

    owner = 2 * x + t
    place = 8 * x + 4 * t + y

    def owner_parts(t2):
        yield 0, dvb.at[t2], vwin.at[pl.ds(pl.multiple_of(128 + y * 256, 128), 256)], 0, (z, owner, t2), None
        yield 1, dvb.at[t2, pl.ds(128, 128)], vwin.at[pl.ds(0, 128)], 1, (z, owner + 1, t2), y == 3
        yield 2, dvb.at[t2, pl.ds(0, 128)], vwin.at[pl.ds(1152, 128)], 2, (z, owner - 1, t2), jnp.logical_and(
            y == 0, owner >= 1
        )
        for k in range(8):
            yield 3 + k, dob.at[t2, pl.ds(32 * k, 64)], owin.at[place], 3, (z, 8 + k, t2), None
        yield 11, dob.at[t2, pl.ds(16, 16)], owin.at[place, pl.ds(48, 16)], 3, (z, 7, t2), None

    def guarded(cond, what):
        if cond is None:
            what()
        else:
            pl.when(cond)(what)

    for t2 in range(2):
        for k, src, dst, r, to, cond in owner_parts(t2):
            guarded(cond, functools.partial(send, src, dst, s_own.at[t2, k], r_own.at[r], to))

    @pl.when(dp <= 7)
    def _():
        wait_bytes(vwin.at[pl.ds(128, 1024)], r_own.at[0])

    @pl.when(jnp.logical_and(dp >= 1, dp <= 8))
    def _():
        wait_bytes(vwin.at[pl.ds(0, 128)], r_own.at[1])

    @pl.when(dp <= 6)
    def _():
        wait_bytes(vwin.at[pl.ds(1152, 128)], r_own.at[2])

    @pl.when(dp == 7)
    def _():
        wait_bytes(owin.at[pl.ds(0, 8)], r_own.at[3])

    @pl.when(dp >= 8)
    def _():
        wait_bytes(owin, r_own.at[3])

    wait_bytes(out, r_out)

    sent(vw, s_wa.at[0], wa_to)
    sent(ow, s_wa.at[1], wa_to)

    @pl.when(x == zl)
    def _():
        for x2 in range(4):
            to = device(x, y, 2 * x2 + zh, t)
            sent(vst, s_w1.at[x2, 0], to)
            sent(ost, s_w1.at[x2, 1], to)

    for k, src, to in x_moves():
        sent(src, s_x.at[k], to)

    @pl.when(top_sender)
    def _():
        for k, src, c, to in top_parts():
            sent(src, s_top.at[k], to)

    for k, src, to in x_parts():
        sent(src, s_xa.at[k], to)
    for k, src, dst, r, to in w2_parts():
        sent(src, s_w2.at[k], to)
    for k, src, to in xd_parts():
        sent(src, s_xd.at[k], to)
    wait_bytes(rsv, s_rsv)
    wait_bytes(rsv, s_agv)
    for k, y2 in y_peers():
        wait_bytes(val.at[y], s_val.at[k])

    def drain(c, carry):
        wait_bytes(rsb.at[c], s_rs.at[c])
        wait_bytes(rsb.at[c], s_ag.at[c])
        for k, src, to in gd_parts(c):
            sent(src, s_gd.at[c, k], to)

        @pl.when(z > 0)
        def _():
            wait_bytes(gout.at[c], s_hop.at[c])

        for k, src, to in out_parts(c):
            sent(src, s_out.at[c, k], to)
        for k, y2 in y_peers():
            wait_bytes(vg.at[y, c], s_vg.at[c, k])
        return carry

    lax.fori_loop(0, CHUNKS, drain, 0)
    for t2 in range(2):
        for k, src, dst, r, to, cond in owner_parts(t2):
            guarded(cond, functools.partial(sent, src, s_own.at[t2, k], to))


def relay(xin, top, vw, ow):
    hbm = pl.BlockSpec(memory_space=pl.ANY)
    dma = pltpu.SemaphoreType.DMA
    return pl.pallas_call(
        relay_kernel,
        out_shape=(
            jax.ShapeDtypeStruct((4, 16, 8192), BF16),
            jax.ShapeDtypeStruct((1280, 256), BF16),
            jax.ShapeDtypeStruct((32, 64, 256), BF16),
        ),
        in_specs=[hbm] * 4,
        out_specs=(hbm, hbm, hbm),
        scratch_shapes=[
            pltpu.VMEM((CHUNKS, 64, 1024), BF16),
            pltpu.VMEM((CHUNKS, 64, 1024), BF16),
            pltpu.VMEM((4, 2, 64, 1024), BF16),
            pltpu.VMEM((4, 4, 32, 1024), BF16),
            pltpu.VMEM((4, 512, 256), BF16),
            pltpu.VMEM((4, 256, 512), BF16),
            pltpu.VMEM((512, 256), BF16),
            pltpu.VMEM((256, 512), BF16),
            pltpu.VMEM((1024, 512), BF16),
            pltpu.VMEM((512, 1024), BF16),
            pltpu.VMEM((CHUNKS, 64, 512), BF16),
            pltpu.VMEM((CHUNKS, 7, 16, 256), BF16),
            pltpu.VMEM((4, CHUNKS, 64, 512), BF16),
            pltpu.VMEM((4, CHUNKS, 64, 256), BF16),
            pltpu.VMEM((512, 512), BF16),
            pltpu.VMEM((7, 128, 256), BF16),
            pltpu.VMEM((4, 512, 512), BF16),
            pltpu.VMEM((4, 4, 2, 64, 256), BF16),
            pltpu.VMEM((256, 512), F32),
            pltpu.VMEM((512, 256), F32),
            pltpu.VMEM((2, 256, 256), BF16),
            pltpu.VMEM((2, 288, 256), BF16),
            dma((8,)), dma((4,)), dma((2,)), dma((4, 2)), dma((8,)), dma((8,)),
            dma((CHUNKS,)), dma((CHUNKS,)), dma((CHUNKS,)), dma((CHUNKS, 4)),
            dma((CHUNKS, 4)), dma((CHUNKS, 3)), dma, dma,
            dma((3,)), dma((4,)), dma((2, 12)),
            dma((4,)), dma, dma((4, 2)), dma((2,)), dma((2,)), dma((CHUNKS,)),
            dma((CHUNKS,)), dma((CHUNKS,)), dma, dma, dma, dma,
            dma, dma, dma((4,)), dma,
        ],
        compiler_params=pltpu.CompilerParams(has_side_effects=True, vmem_limit_bytes=48 * 1024 * 1024),
    )(xin, top, vw, ow)


def adam_kernel(steps, lengths, vwin, owin, param, first, second, new_param, new_first, new_second, flat):
    dp = lax.axis_index("dp")
    step = pl.program_id(0)
    rows = param.shape[0]

    def from_value(low, high):
        for a in range(low, high, 128):
            part = vwin[a : a + 128, :].astype(F32)
            flat[pl.ds(2 * a, 128, stride=2), :] = part[:, :128]
            flat[pl.ds(2 * a + 1, 128, stride=2), :] = part[:, 128:]

    def from_output(low, high):
        for e in range(32):
            part = owin[e].astype(F32)[12 + low : 12 + high, :]
            for h in range(2):
                flat[pl.ds(low * 64 + e * 2 + h, high - low, stride=64), :] = part[:, h * 128 : h * 128 + 128]

    @pl.when(step == 0)
    def _():
        flat[2560:, :] = jnp.zeros((flat.shape[0] - 2560, 128), F32)
        for last, value_rows, output_rows in ((8, (0, 128), (0, 4)), (7, (128, 1152), (4, 36)), (6, (1152, 1280), (36, 40))):
            pl.when(dp <= last)(functools.partial(from_value, *value_rows))
            pl.when(dp > last)(functools.partial(from_output, *output_rows))

    start = lax.fori_loop(0, dp, lambda e, total: total + lengths[e], jnp.int32(0))
    length = lengths[dp]
    offset = start - dp * 262144 + 32768
    row, lane = lax.div(offset, 128), lax.rem(offset, 128)
    window = flat[pl.ds(step * rows + row, rows + 8), :]
    turned = pltpu.roll(window, lax.rem(128 - lane, 128), 1)
    lanes = lax.broadcasted_iota(jnp.int32, (rows, 128), 1)
    grad = jnp.where(lanes < 128 - lane, turned[:rows], turned[1 : rows + 1])
    index = (step * rows + lax.broadcasted_iota(jnp.int32, (rows, 128), 0)) * 128 + lanes
    grad = jnp.where(index < length, grad, 0.0)

    first_new = beta_one * first[...] + (1.0 - beta_one) * grad
    second_new = beta_two * second[...] + (1.0 - beta_two) * grad * grad
    corrected = (
        first_new
        / (1.0 - beta_one**adam_step)
        / (jnp.sqrt(second_new / (1.0 - beta_two**adam_step)) + adam_eps)
    )
    new_param[...] = param[...] - learn_rate * (corrected + decay_rate * param[...])
    new_first[...] = first_new
    new_second[...] = second_new


def adam(lengths, vwin, owin, param, first, second):
    steps = 5
    block = pl.BlockSpec((2560 // steps, 128), lambda i: (i, 0))
    shape = jax.ShapeDtypeStruct((2560, 128), F32)
    return pl.pallas_call(
        functools.partial(adam_kernel, steps),
        grid=(steps,),
        out_shape=(shape, shape, shape),
        in_specs=[
            pl.BlockSpec(memory_space=pltpu.SMEM),
            pl.BlockSpec(memory_space=pltpu.VMEM),
            pl.BlockSpec(memory_space=pltpu.VMEM),
            block,
            block,
            block,
        ],
        out_specs=(block, block, block),
        scratch_shapes=[pltpu.VMEM((2560 + 528, 128), F32)],
        compiler_params=pltpu.CompilerParams(vmem_limit_bytes=32 * 1024 * 1024),
    )(lengths, vwin, owin, param, first, second)


def local(section_inputs, top_grad, value_weight, output_weight, owner_lengths, master_param, moment1, moment2):
    out, vwin, owin = relay(section_inputs[0], top_grad, value_weight[0], output_weight[0])
    flat = (2560, 128)
    updated = adam(
        owner_lengths[0, 0], vwin, owin, master_param.reshape(flat), moment1.reshape(flat), moment2.reshape(flat)
    )
    return (out[None], *(array.reshape(1, 1, -1) for array in updated))


def solution(mesh):
    in_specs = (
        P("section", None, ("dp", "tensor"), None),
        P(None, ("dp", "tensor"), None),
        P("section", "dp", "tensor"),
        P("section", "tensor", "dp"),
        P("section", "tensor", None),
        P("section", "tensor", "dp"),
        P("section", "tensor", "dp"),
        P("section", "tensor", "dp"),
    )
    out_specs = (
        P("section", None, ("dp", "tensor"), None),
        P("section", "tensor", "dp"),
        P("section", "tensor", "dp"),
        P("section", "tensor", "dp"),
    )
    return jax.shard_map(local, mesh=mesh, in_specs=in_specs, out_specs=out_specs, check_vma=False)
```

```python
import functools
import math

import jax
import jax.numpy as jnp
from jax import lax
from jax.experimental import pallas as pl
from jax.experimental.pallas import tpu as pltpu
from jax.sharding import PartitionSpec as P

MESH = pl.DeviceIdType.MESH
BF16 = jnp.bfloat16
F32 = jnp.float32

beta_one = 0.9
beta_two = 0.95
learn_rate = 0.001
decay_rate = 0.1
adam_eps = 1e-08
adam_step = 20.0

CHUNKS = 8
ROWS = 512 // CHUNKS
PIECE = ROWS // 4
MOVE_AT = 2
NT = (((1,), (1,)), ((), ()))
NN = (((1,), (0,)), ((), ()))
TN = (((0,), (0,)), ((), ()))


def dot(a, b, dims):
    return lax.dot_general(a, b, dims, preferred_element_type=F32)


def device(x, y, z, t):
    return (2 * x + lax.div(z, 4), lax.rem(z, 4) * 4 + y, t)


def aligned(start, size):
    return pl.ds(pl.multiple_of(start, size), size)


def wait_bytes(ref, sem):
    pltpu.make_async_copy(ref, ref, sem).wait()


def relay_kernel(
    xin, top, vw, ow,
    out, vwin, owin,
    gtop, gin, gout, xrow, xst, vwst, owst, vst, ost, vd, od, pbuf, rsb, vgo, vg, gd, pv, rsv, val, xd,
    accv, acco, dvb, dob, mid,
    s_xa, s_x, s_wa, s_w1, s_w2, s_top, s_rs, s_ag, s_hop, s_out, s_gd, s_vg, s_rsv, s_agv, s_val, s_xd,
    s_own, s_mid, s_fin,
    r_xa, r_x, r_wa, r_w1, r_w2, r_top, r_g, r_rs, r_ag, r_gd, r_vg, r_rsv, r_agv, r_val, r_xd, r_own, r_mid, r_out,
):
    sec = lax.axis_index("section")
    dp = lax.axis_index("dp")
    t = lax.axis_index("tensor")
    x = lax.div(sec, 2)
    zh = lax.rem(sec, 2)
    zl = lax.div(dp, 4)
    y = lax.rem(dp, 4)
    z = zh * 4 + zl
    after = lax.rem(z + 1, 8)
    below = lax.rem(z + 7, 8)

    def is_me(to):
        return jnp.logical_and(jnp.logical_and(to[0] == sec, to[1] == dp), to[2] == t)

    def send(src, dst, ssem, rsem, to):
        mine = is_me(to)

        @pl.when(mine)
        def _():
            pltpu.make_async_copy(src, dst, rsem).start()

        @pl.when(jnp.logical_not(mine))
        def _():
            pltpu.make_async_remote_copy(src, dst, ssem, rsem, device_id=to, device_id_type=MESH).start()

    def sent(src, ssem, to):
        @pl.when(jnp.logical_not(is_me(to)))
        def _():
            wait_bytes(src, ssem)

    def push(src, dst, ssem, rsem, to):
        pltpu.make_async_remote_copy(src, dst, ssem, rsem, device_id=to, device_id_type=MESH).start()

    wa_to = device(zl, y, z, t)
    send(ow, owst.at[x], s_wa.at[1], r_wa.at[x, 1], wa_to)

    def top_parts():
        for mb in range(4):
            for t2 in range(2):
                row = mb * 128 + zl * 32 + t * 16
                c, rest = lax.div(row, ROWS), lax.rem(row, ROWS)
                src = top.at[mb, :, aligned(x * 2048 + t2 * 1024, 1024)]
                yield mb * 2 + t2, src, gtop.at[c, aligned(rest, 16), :], c, device(x, y, 7, t2)

    top_sender = jnp.logical_or(z < 2, z >= 6)

    @pl.when(top_sender)
    def _():
        for k, src, dst, c, to in top_parts():
            send(src, dst, s_top.at[k], r_top.at[c], to)

    send(vw, vwst.at[x], s_wa.at[0], r_wa.at[x, 0], wa_to)

    def w1_parts(which):
        for x2 in reversed(range(4)):
            plane = 2 * x2 + zh
            if which:
                yield x2, owst.at[x2], ost, device(x, y, plane, t)
            else:
                yield x2, vwst.at[x2], vst, device(x, y, lax.rem(plane + 7, 8), t)

    def w2_parts(which):
        rows = aligned(lax.rem(y, 2) * 512, 512)
        cols = aligned(t * 256, 256)
        for y2 in range(4):
            to = device(x, y2, z, lax.div(y, 2))
            if which:
                yield y2, ost, od.at[cols, rows], to
            else:
                yield y2, vst, vd.at[rows, cols], to

    def x_parts():
        for x2 in range(4):
            for t2 in range(2):
                yield x2 * 2 + t2, xin.at[:, :, pl.ds(x2 * 2048 + t2 * 1024, 1024)], device(x2, y, z, t2)

    def x_moves():
        for x2 in reversed(range(4)):
            yield x2, xst.at[x2], device(x, y, lax.rem(2 * x2 + zh + 7, 8), t)

    def move_inputs():
        for k, src, to in x_moves():
            wait_bytes(src, r_xa.at[k])
            send(src, xrow.at[:, aligned(zl * 32, 32), :], s_x.at[k], r_x, to)

    for which in (1, 0):

        @pl.when(x == zl)
        def _():
            for k, src, dst, to in w1_parts(which):
                wait_bytes(src, r_wa.at[k, which])
                send(src, dst, s_w1.at[k, which], r_w1.at[which], to)

        wait_bytes(ost if which else vst, r_w1.at[which])
        for k, src, dst, to in w2_parts(which):
            send(src, dst, s_w2.at[k, which], r_w2.at[which], to)
    for k, src, to in x_parts():
        send(src, xst.at[x, :, aligned(t * 16, 16), :], s_xa.at[k], r_xa.at[x], to)
    wait_bytes(od, r_w2.at[1])

    def peers():
        for k in range(1, 8):
            yield k - 1, lax.rem(x + k // 2, 4), lax.rem(t + k % 2, 2)

    def y_peers():
        for k in range(1, 4):
            yield k - 1, lax.rem(y + k, 4)

    def multiply(ref, c):
        pbuf[c] = dot(ref[c], od[...], NT).astype(BF16)
        for k, x2, t2 in peers():
            push(
                pbuf.at[c, aligned(x2 * PIECE, PIECE), aligned(t2 * 256, 256)],
                rsb.at[c, k],
                s_rs.at[c],
                r_rs.at[c],
                device(x2, y, z, t2),
            )

    def add_up(c):
        rows, cols = aligned(x * PIECE, PIECE), aligned(t * 256, 256)
        wait_bytes(rsb.at[c], r_rs.at[c])
        total = pbuf[c, rows, cols].astype(F32)
        for k in range(7):
            total = total + rsb[c, k].astype(F32)
        vgo[c] = total.astype(BF16)
        for k in range(8):
            to = device(lax.rem(x + k // 2, 4), y, below, lax.rem(t + k % 2, 2))
            push(vgo.at[c], vg.at[y, c, rows, cols], s_ag.at[c], r_ag.at[c], to)

    def add_branch(c):
        wait_bytes(gin.at[c], r_g.at[c])
        wait_bytes(vg.at[y, c], r_ag.at[c])
        branch = dot(vg[y, c], vd[...], NT)
        gout[c] = (gin[c].astype(F32) + branch).astype(BF16)

    def gd_parts(c):
        for y2 in range(4):
            yield y2, gin.at[c, :, pl.ds(y2 * 256, 256)], device(x, y2, z, t)

    def out_parts(c):
        for a in range(ROWS // 16):
            row = c * ROWS + a * 16
            mb, z2, t2 = lax.div(row, 128), lax.rem(lax.div(row, 32), 4), a % 2
            dst = out.at[mb, :, aligned(x * 2048 + t * 1024, 1024)]
            yield a, gout.at[c, pl.ds(a * 16, 16), :], dst, (after, z2 * 4 + y, t2)

    def hand_out(c):
        for k, src, dst, to in out_parts(c):
            send(src, dst, s_out.at[c, k], r_out, to)
        for k, y2 in y_peers():
            push(vg.at[y, c], vg.at[y, c], s_vg.at[c, k], r_vg, device(x, y2, z, t))
        for k, src, to in gd_parts(c):
            send(src, gd.at[y, c], s_gd.at[c, k], r_gd, to)

    def xd_parts():
        for y2 in range(4):
            yield y2, xrow.at[:, :, pl.ds(y2 * 256, 256)], device(x, y2, z, t)

    def values_stage():
        wait_bytes(xrow, r_x)
        for k, src, to in xd_parts():
            send(src, xd.at[y], s_xd.at[k], r_xd, to)

        def block(i, carry):
            pv[aligned(i * 128, 128), :] = dot(xrow[i], vd[...], NN).astype(BF16)
            return carry

        lax.fori_loop(0, 4, block, 0)
        for k, x2, t2 in peers():
            push(
                pv.at[aligned(x2 * 128, 128), aligned(t2 * 256, 256)], rsv.at[k], s_rsv, r_rsv, device(x2, y, z, t2)
            )
        wait_bytes(rsv, r_rsv)
        rows, cols = aligned(x * 128, 128), aligned(t * 256, 256)
        total = pv[rows, cols].astype(F32)
        for k in range(7):
            total = total + rsv[k].astype(F32)
        val[y, rows, cols] = total.astype(BF16)
        mine = val.at[y, rows, cols]
        for k, x2, t2 in peers():
            push(mine, mine, s_agv, r_agv, device(x2, y, z, t2))
        wait_bytes(rsv, r_agv)
        for k, y2 in y_peers():
            push(val.at[y], val.at[y], s_val.at[k], r_val, device(x, y2, z, t))

    @pl.when(z == 7)
    def _():
        def begin(c):
            wait_bytes(gtop.at[c], r_top.at[c])
            push(gtop.at[c], gin.at[c], s_hop.at[c], r_g.at[c], device(x, y, below, t))
            multiply(gtop, c)

        def step(c, carry):
            pl.when(c + 1 < CHUNKS)(lambda: begin(c + 1))
            pl.when(c == MOVE_AT)(move_inputs)
            add_up(c)
            return carry

        begin(0)
        lax.fori_loop(0, CHUNKS, step, 0)
        wait_bytes(vd, r_w2.at[0])

    @pl.when(z < 7)
    def _():
        move_inputs()
        wait_bytes(vd, r_w2.at[0])
        pl.when(z < 2)(values_stage)

        def step(c, carry):
            add_branch(c)
            push(gout.at[c], gin.at[c], s_hop.at[c], r_g.at[c], device(x, y, below, t))
            multiply(gout, c)
            hand_out(c)
            add_up(c)
            return carry

        lax.fori_loop(0, CHUNKS, step, 0)

    pl.when(z >= 2)(values_stage)

    @pl.when(z == 7)
    def _():
        def step(c, carry):
            add_branch(c)
            hand_out(c)
            return carry

        lax.fori_loop(0, CHUNKS, step, 0)

    wait_bytes(xd, r_xd)
    wait_bytes(val.at[pl.ds(0, 3)], r_val)
    wait_bytes(gd, r_gd)
    wait_bytes(vg.at[pl.ds(0, 3)], r_vg)
    accv[...] = jnp.zeros_like(accv)
    acco[...] = jnp.zeros_like(acco)

    def grad_step(j, carry):
        accv[...] += dot(xd[j].reshape(512, 256), vg[j].reshape(512, 512), TN)
        acco[...] += dot(val[j], gd[j].reshape(512, 256), TN)
        return carry

    lax.fori_loop(0, 4, grad_step, 0)
    scale = 1.0 / math.sqrt(2048)
    for t2 in range(2):
        dvb[t2] = (accv[:, t2 * 256 : t2 * 256 + 256] * scale).astype(BF16)
        dob[t2, 0:16, :] = jnp.zeros((16, 256), BF16)
        dob[t2, 16:272, :] = (acco[t2 * 256 : t2 * 256 + 256, :] * scale).astype(BF16)
        dob[t2, 272:288, :] = jnp.zeros((16, 256), BF16)

    owner = 2 * x + t
    place = 8 * x + 4 * t + y
    half = lax.rem(after, 2)

    def mid_parts():
        for t2 in range(2):
            for q in range(2):
                dst = mid.at[lax.div(after, 2), t2]
                yield t2, q, dob.at[t2, pl.ds(128 * q, 160)], dst, device(x, y, 4 * half + 2 + q, t)

    def owner_parts():
        for t2 in range(2):
            main = vwin.at[pl.ds(pl.multiple_of(128 + y * 256, 128), 256)]
            yield t2, 0, dvb.at[t2], main, (after, owner, t2), None
            yield t2, 1, dvb.at[t2, pl.ds(128, 128)], vwin.at[pl.ds(0, 128)], (after, owner + 1, t2), y == 3
            low = jnp.logical_and(y == 0, owner >= 1)
            yield t2, 2, dvb.at[t2, pl.ds(0, 128)], vwin.at[pl.ds(1152, 128)], (after, owner - 1, t2), low
            yield t2, 3, dob.at[t2, pl.ds(16, 16)], owin.at[place, pl.ds(48, 16)], (after, 7, t2), None

    def fin_parts(j):
        for t2 in range(2):
            for y2 in range(4):
                to = (2 * j + zh, zl * 4 + y2, t2)
                yield t2 * 4 + y2, mid.at[j, t2, pl.ds(32 * y2, 64)], owin.at[place], to

    def guarded(cond, what):
        if cond is None:
            what()
        else:
            pl.when(cond)(what)

    for t2, q, src, dst, to in mid_parts():
        send(src, dst, s_mid.at[t2, q], r_mid.at[lax.div(after, 2), t2], to)
    for t2, k, src, dst, to, cond in owner_parts():
        guarded(cond, functools.partial(send, src, dst, s_own.at[t2, k], r_own.at[k], to))

    @pl.when(zl >= 2)
    def _():
        for j in reversed(range(4)):
            for t2 in range(2):
                wait_bytes(mid.at[j, t2], r_mid.at[j, t2])
            for k, src, dst, to in fin_parts(j):
                send(src, dst, s_fin.at[j, k], r_own.at[3], to)

    @pl.when(dp <= 7)
    def _():
        wait_bytes(vwin.at[pl.ds(128, 1024)], r_own.at[0])

    @pl.when(jnp.logical_and(dp >= 1, dp <= 8))
    def _():
        wait_bytes(vwin.at[pl.ds(0, 128)], r_own.at[1])

    @pl.when(dp <= 6)
    def _():
        wait_bytes(vwin.at[pl.ds(1152, 128)], r_own.at[2])

    @pl.when(dp == 7)
    def _():
        wait_bytes(owin.at[pl.ds(0, 8)], r_own.at[3])

    @pl.when(dp >= 8)
    def _():
        wait_bytes(owin, r_own.at[3])

    wait_bytes(out, r_out)

    sent(vw, s_wa.at[0], wa_to)
    sent(ow, s_wa.at[1], wa_to)

    @pl.when(top_sender)
    def _():
        for k, src, dst, c, to in top_parts():
            sent(src, s_top.at[k], to)

    for which in (1, 0):

        @pl.when(x == zl)
        def _():
            for k, src, dst, to in w1_parts(which):
                sent(src, s_w1.at[k, which], to)

        for k, src, dst, to in w2_parts(which):
            sent(src, s_w2.at[k, which], to)
    for k, src, to in x_moves():
        sent(src, s_x.at[k], to)
    for k, src, to in x_parts():
        sent(src, s_xa.at[k], to)
    for k, src, to in xd_parts():
        sent(src, s_xd.at[k], to)
    wait_bytes(rsv, s_rsv)
    wait_bytes(rsv, s_agv)
    for k, y2 in y_peers():
        wait_bytes(val.at[y], s_val.at[k])

    def drain(c, carry):
        wait_bytes(rsb.at[c], s_rs.at[c])
        wait_bytes(vg.at[y, c], s_ag.at[c])
        wait_bytes(gout.at[c], s_hop.at[c])
        for k, src, to in gd_parts(c):
            sent(src, s_gd.at[c, k], to)
        for k, src, dst, to in out_parts(c):
            sent(src, s_out.at[c, k], to)
        for k, y2 in y_peers():
            wait_bytes(vg.at[y, c], s_vg.at[c, k])
        return carry

    lax.fori_loop(0, CHUNKS, drain, 0)
    for t2, q, src, dst, to in mid_parts():
        sent(src, s_mid.at[t2, q], to)
    for t2, k, src, dst, to, cond in owner_parts():
        guarded(cond, functools.partial(sent, src, s_own.at[t2, k], to))

    @pl.when(zl >= 2)
    def _():
        for j in range(4):
            for k, src, dst, to in fin_parts(j):
                sent(src, s_fin.at[j, k], to)


def relay(xin, top, vw, ow):
    hbm = pl.BlockSpec(memory_space=pl.ANY)
    dma = pltpu.SemaphoreType.DMA
    return pl.pallas_call(
        relay_kernel,
        out_shape=(
            jax.ShapeDtypeStruct((4, 16, 8192), BF16),
            jax.ShapeDtypeStruct((1280, 256), BF16),
            jax.ShapeDtypeStruct((32, 64, 256), BF16),
        ),
        in_specs=[hbm] * 4,
        out_specs=(hbm, hbm, hbm),
        scratch_shapes=[
            pltpu.VMEM((CHUNKS, ROWS, 1024), BF16),
            pltpu.VMEM((CHUNKS, ROWS, 1024), BF16),
            pltpu.VMEM((CHUNKS, ROWS, 1024), BF16),
            pltpu.VMEM((4, 128, 1024), BF16),
            pltpu.VMEM((4, 4, 32, 1024), BF16),
            pltpu.VMEM((4, 512, 256), BF16),
            pltpu.VMEM((4, 256, 512), BF16),
            pltpu.VMEM((512, 256), BF16),
            pltpu.VMEM((256, 512), BF16),
            pltpu.VMEM((1024, 512), BF16),
            pltpu.VMEM((512, 1024), BF16),
            pltpu.VMEM((CHUNKS, ROWS, 512), BF16),
            pltpu.VMEM((CHUNKS, 7, PIECE, 256), BF16),
            pltpu.VMEM((CHUNKS, PIECE, 256), BF16),
            pltpu.VMEM((4, CHUNKS, ROWS, 512), BF16),
            pltpu.VMEM((4, CHUNKS, ROWS, 256), BF16),
            pltpu.VMEM((512, 512), BF16),
            pltpu.VMEM((7, 128, 256), BF16),
            pltpu.VMEM((4, 512, 512), BF16),
            pltpu.VMEM((4, 4, 128, 256), BF16),
            pltpu.VMEM((256, 512), F32),
            pltpu.VMEM((512, 256), F32),
            pltpu.VMEM((2, 256, 256), BF16),
            pltpu.VMEM((2, 288, 256), BF16),
            pltpu.VMEM((4, 2, 160, 256), BF16),
            dma((8,)), dma((4,)), dma((2,)), dma((4, 2)), dma((4, 2)), dma((8,)),
            dma((CHUNKS,)), dma((CHUNKS,)), dma((CHUNKS,)), dma((CHUNKS, ROWS // 16)),
            dma((CHUNKS, 4)), dma((CHUNKS, 3)), dma, dma,
            dma((3,)), dma((4,)), dma((2, 4)), dma((2, 2)), dma((4, 8)),
            dma((4,)), dma, dma((4, 2)), dma((2,)), dma((2,)),
            dma((CHUNKS,)), dma((CHUNKS,)), dma((CHUNKS,)), dma((CHUNKS,)),
            dma, dma, dma, dma, dma, dma,
            dma((4,)), dma((4, 2)), dma,
        ],
        compiler_params=pltpu.CompilerParams(has_side_effects=True, vmem_limit_bytes=48 * 1024 * 1024),
    )(xin, top, vw, ow)


def adam_kernel(steps, lengths, vwin, owin, param, first, second, new_param, new_first, new_second, flat):
    dp = lax.axis_index("dp")
    step = pl.program_id(0)
    rows = param.shape[0]

    def from_value(low, high):
        for a in range(low, high, 128):
            part = vwin[a : a + 128, :].astype(F32)
            flat[pl.ds(2 * a, 128, stride=2), :] = part[:, :128]
            flat[pl.ds(2 * a + 1, 128, stride=2), :] = part[:, 128:]

    def from_output(low, high):
        for e in range(32):
            part = owin[e].astype(F32)[12 + low : 12 + high, :]
            for h in range(2):
                flat[pl.ds(low * 64 + e * 2 + h, high - low, stride=64), :] = part[:, h * 128 : h * 128 + 128]

    @pl.when(step == 0)
    def _():
        flat[2560:, :] = jnp.zeros((flat.shape[0] - 2560, 128), F32)
        for last, value_rows, output_rows in ((8, (0, 128), (0, 4)), (7, (128, 1152), (4, 36)), (6, (1152, 1280), (36, 40))):
            pl.when(dp <= last)(functools.partial(from_value, *value_rows))
            pl.when(dp > last)(functools.partial(from_output, *output_rows))

    start = lax.fori_loop(0, dp, lambda e, total: total + lengths[e], jnp.int32(0))
    length = lengths[dp]
    offset = start - dp * 262144 + 32768
    row, lane = lax.div(offset, 128), lax.rem(offset, 128)
    window = flat[pl.ds(step * rows + row, rows + 8), :]
    turned = pltpu.roll(window, lax.rem(128 - lane, 128), 1)
    lanes = lax.broadcasted_iota(jnp.int32, (rows, 128), 1)
    grad = jnp.where(lanes < 128 - lane, turned[:rows], turned[1 : rows + 1])
    index = (step * rows + lax.broadcasted_iota(jnp.int32, (rows, 128), 0)) * 128 + lanes
    grad = jnp.where(index < length, grad, 0.0)

    first_new = beta_one * first[...] + (1.0 - beta_one) * grad
    second_new = beta_two * second[...] + (1.0 - beta_two) * grad * grad
    corrected = (
        first_new
        / (1.0 - beta_one**adam_step)
        / (jnp.sqrt(second_new / (1.0 - beta_two**adam_step)) + adam_eps)
    )
    new_param[...] = param[...] - learn_rate * (corrected + decay_rate * param[...])
    new_first[...] = first_new
    new_second[...] = second_new


def adam(lengths, vwin, owin, param, first, second):
    steps = 5
    block = pl.BlockSpec((2560 // steps, 128), lambda i: (i, 0))
    shape = jax.ShapeDtypeStruct((2560, 128), F32)
    return pl.pallas_call(
        functools.partial(adam_kernel, steps),
        grid=(steps,),
        out_shape=(shape, shape, shape),
        in_specs=[
            pl.BlockSpec(memory_space=pltpu.SMEM),
            pl.BlockSpec(memory_space=pltpu.VMEM),
            pl.BlockSpec(memory_space=pltpu.VMEM),
            block,
            block,
            block,
        ],
        out_specs=(block, block, block),
        scratch_shapes=[pltpu.VMEM((2560 + 528, 128), F32)],
        compiler_params=pltpu.CompilerParams(vmem_limit_bytes=32 * 1024 * 1024),
    )(lengths, vwin, owin, param, first, second)


def local(section_inputs, top_grad, value_weight, output_weight, owner_lengths, master_param, moment1, moment2):
    out, vwin, owin = relay(section_inputs[0], top_grad, value_weight[0], output_weight[0])
    flat = (2560, 128)
    updated = adam(
        owner_lengths[0, 0], vwin, owin, master_param.reshape(flat), moment1.reshape(flat), moment2.reshape(flat)
    )
    return (out[None], *(array.reshape(1, 1, -1) for array in updated))


def solution(mesh):
    in_specs = (
        P("section", None, ("dp", "tensor"), None),
        P(None, ("dp", "tensor"), None),
        P("section", "dp", "tensor"),
        P("section", "tensor", "dp"),
        P("section", "tensor", None),
        P("section", "tensor", "dp"),
        P("section", "tensor", "dp"),
        P("section", "tensor", "dp"),
    )
    out_specs = (
        P("section", None, ("dp", "tensor"), None),
        P("section", "tensor", "dp"),
        P("section", "tensor", "dp"),
        P("section", "tensor", "dp"),
    )
    return jax.shard_map(local, mesh=mesh, in_specs=in_specs, out_specs=out_specs, check_vma=False)
```

```python
import functools
import math

import jax
import jax.numpy as jnp
from jax import lax
from jax.experimental import pallas as pl
from jax.experimental.pallas import tpu as pltpu
from jax.sharding import PartitionSpec as P

MESH = pl.DeviceIdType.MESH
BF16 = jnp.bfloat16
F32 = jnp.float32

beta_one = 0.9
beta_two = 0.95
learn_rate = 0.001
decay_rate = 0.1
adam_eps = 1e-08
adam_step = 20.0

CHUNKS = 8
ROWS = 512 // CHUNKS
PIECE = ROWS // 4
PACED = 2
GO_AT = 7
MOVE_AT = 7
NT = (((1,), (1,)), ((), ()))
NN = (((1,), (0,)), ((), ()))
TN = (((0,), (0,)), ((), ()))


def dot(a, b, dims):
    return lax.dot_general(a, b, dims, preferred_element_type=F32)


def device(x, y, z, t):
    return (2 * x + lax.div(z, 4), lax.rem(z, 4) * 4 + y, t)


def aligned(start, size):
    return pl.ds(pl.multiple_of(start, size), size)


def wait_bytes(ref, sem):
    pltpu.make_async_copy(ref, ref, sem).wait()


def relay_kernel(
    xin, top, vw, ow,
    out, vwin, owin,
    gtop, gin, gout, xrow, xst, vwst, owst, vst, ost, vd, od, pbuf, rsb, vgo, vg, gd, pv, rsv, val, xd,
    accv, acco, dvb, dob, mid,
    s_xa, s_x, s_wa, s_w1, s_w2, s_top, s_rs, s_ag, s_hop, s_out, s_gd, s_vg, s_rsv, s_agv, s_val, s_xd,
    s_own, s_mid, s_fin,
    r_xa, r_x, r_wa, r_w1, r_w2, r_top, r_g, r_rs, r_ag, r_gd, r_vg, r_rsv, r_agv, r_val, r_xd, r_own, r_mid, r_out, go,
):
    sec = lax.axis_index("section")
    dp = lax.axis_index("dp")
    t = lax.axis_index("tensor")
    x = lax.div(sec, 2)
    zh = lax.rem(sec, 2)
    zl = lax.div(dp, 4)
    y = lax.rem(dp, 4)
    z = zh * 4 + zl
    after = lax.rem(z + 1, 8)
    below = lax.rem(z + 7, 8)

    def is_me(to):
        return jnp.logical_and(jnp.logical_and(to[0] == sec, to[1] == dp), to[2] == t)

    def send(src, dst, ssem, rsem, to):
        mine = is_me(to)

        @pl.when(mine)
        def _():
            pltpu.make_async_copy(src, dst, rsem).start()

        @pl.when(jnp.logical_not(mine))
        def _():
            pltpu.make_async_remote_copy(src, dst, ssem, rsem, device_id=to, device_id_type=MESH).start()

    def sent(src, ssem, to):
        @pl.when(jnp.logical_not(is_me(to)))
        def _():
            wait_bytes(src, ssem)

    def push(src, dst, ssem, rsem, to):
        pltpu.make_async_remote_copy(src, dst, ssem, rsem, device_id=to, device_id_type=MESH).start()

    wa_to = device(zl, y, z, t)
    send(ow, owst.at[x], s_wa.at[1], r_wa.at[x, 1], wa_to)

    def top_parts():
        for mb in range(4):
            for t2 in range(2):
                row = mb * 128 + zl * 32 + t * 16
                c, rest = lax.div(row, ROWS), lax.rem(row, ROWS)
                src = top.at[mb, :, aligned(x * 2048 + t2 * 1024, 1024)]
                yield mb * 2 + t2, src, gtop.at[c, aligned(rest, 16), :], c, device(x, y, 7, t2)

    top_sender = jnp.logical_or(z < 2, z >= 6)

    @pl.when(top_sender)
    def _():
        for k, src, dst, c, to in top_parts():
            send(src, dst, s_top.at[k], r_top.at[c], to)

    send(vw, vwst.at[x], s_wa.at[0], r_wa.at[x, 0], wa_to)

    def w1_parts(which):
        for x2 in reversed(range(4)):
            plane = 2 * x2 + zh
            if which:
                yield x2, owst.at[x2], ost, device(x, y, plane, t)
            else:
                yield x2, vwst.at[x2], vst, device(x, y, lax.rem(plane + 7, 8), t)

    def w2_parts(which):
        rows = aligned(lax.rem(y, 2) * 512, 512)
        cols = aligned(t * 256, 256)
        for y2 in range(4):
            to = device(x, y2, z, lax.div(y, 2))
            if which:
                yield y2, ost, od.at[cols, rows], to
            else:
                yield y2, vst, vd.at[rows, cols], to

    def x_parts():
        for x2 in range(4):
            for t2 in range(2):
                yield x2 * 2 + t2, xin.at[:, :, pl.ds(x2 * 2048 + t2 * 1024, 1024)], device(x2, y, z, t2)

    def x_moves():
        for x2 in reversed(range(4)):
            yield x2, xst.at[x2], device(x, y, lax.rem(2 * x2 + zh + 7, 8), t)

    def move_inputs():
        for k, src, to in x_moves():
            wait_bytes(src, r_xa.at[k])
            send(src, xrow.at[:, aligned(zl * 32, 32), :], s_x.at[k], r_x, to)

    for which in (1, 0):

        @pl.when(x == zl)
        def _():
            for k, src, dst, to in w1_parts(which):
                wait_bytes(src, r_wa.at[k, which])
                send(src, dst, s_w1.at[k, which], r_w1.at[which], to)

        wait_bytes(ost if which else vst, r_w1.at[which])
        for k, src, dst, to in w2_parts(which):
            send(src, dst, s_w2.at[k, which], r_w2.at[which], to)
    for k, src, to in x_parts():
        send(src, xst.at[x, :, aligned(t * 16, 16), :], s_xa.at[k], r_xa.at[x], to)
    wait_bytes(od, r_w2.at[1])

    def peers():
        for k in range(1, 8):
            yield k - 1, lax.rem(x + k // 2, 4), lax.rem(t + k % 2, 2)

    def y_peers():
        for k in range(1, 4):
            yield k - 1, lax.rem(y + k, 4)

    def multiply(ref, c):
        pbuf[c] = dot(ref[c], od[...], NT).astype(BF16)
        for k, x2, t2 in peers():
            push(
                pbuf.at[c, aligned(x2 * PIECE, PIECE), aligned(t2 * 256, 256)],
                rsb.at[c, k],
                s_rs.at[c],
                r_rs.at[c],
                device(x2, y, z, t2),
            )

    def add_up(c):
        rows, cols = aligned(x * PIECE, PIECE), aligned(t * 256, 256)
        wait_bytes(rsb.at[c], r_rs.at[c])
        total = pbuf[c, rows, cols].astype(F32)
        for k in range(7):
            total = total + rsb[c, k].astype(F32)
        vgo[c] = total.astype(BF16)
        for k in range(8):
            to = device(lax.rem(x + k // 2, 4), y, below, lax.rem(t + k % 2, 2))
            push(vgo.at[c], vg.at[y, c, rows, cols], s_ag.at[c], r_ag.at[c], to)

    def add_branch(c):
        wait_bytes(gin.at[c], r_g.at[c])
        wait_bytes(vg.at[y, c], r_ag.at[c])
        branch = dot(vg[y, c], vd[...], NT)
        gout[c] = (gin[c].astype(F32) + branch).astype(BF16)

    def gd_parts(c):
        for y2 in range(4):
            yield y2, gin.at[c, :, pl.ds(y2 * 256, 256)], device(x, y2, z, t)

    def out_parts(c):
        for a in range(ROWS // 16):
            row = c * ROWS + a * 16
            mb, z2, t2 = lax.div(row, 128), lax.rem(lax.div(row, 32), 4), a % 2
            dst = out.at[mb, :, aligned(x * 2048 + t * 1024, 1024)]
            yield a, gout.at[c, pl.ds(a * 16, 16), :], dst, (after, z2 * 4 + y, t2)

    def rows_out(c):
        for k, src, dst, to in out_parts(c):
            send(src, dst, s_out.at[c, k], r_out, to)

    def hand_out(c):
        rows_out(c)
        hand_in(c)

    def hand_in(c):
        for k, y2 in y_peers():
            push(vg.at[y, c], vg.at[y, c], s_vg.at[c, k], r_vg, device(x, y2, z, t))
        for k, src, to in gd_parts(c):
            send(src, gd.at[y, c], s_gd.at[c, k], r_gd, to)

    def xd_parts():
        for y2 in range(4):
            yield y2, xrow.at[:, :, pl.ds(y2 * 256, 256)], device(x, y2, z, t)

    def values_stage():
        wait_bytes(xrow, r_x)
        for k, src, to in xd_parts():
            send(src, xd.at[y], s_xd.at[k], r_xd, to)

        def block(i, carry):
            pv[aligned(i * 128, 128), :] = dot(xrow[i], vd[...], NN).astype(BF16)
            return carry

        lax.fori_loop(0, 4, block, 0)
        for k, x2, t2 in peers():
            push(
                pv.at[aligned(x2 * 128, 128), aligned(t2 * 256, 256)], rsv.at[k], s_rsv, r_rsv, device(x2, y, z, t2)
            )
        wait_bytes(rsv, r_rsv)
        rows, cols = aligned(x * 128, 128), aligned(t * 256, 256)
        total = pv[rows, cols].astype(F32)
        for k in range(7):
            total = total + rsv[k].astype(F32)
        val[y, rows, cols] = total.astype(BF16)
        mine = val.at[y, rows, cols]
        for k, x2, t2 in peers():
            push(mine, mine, s_agv, r_agv, device(x2, y, z, t2))
        wait_bytes(rsv, r_agv)
        for k, y2 in y_peers():
            push(val.at[y], val.at[y], s_val.at[k], r_val, device(x, y2, z, t))

    @pl.when(z == 7)
    def _():
        def begin(c):
            wait_bytes(gtop.at[c], r_top.at[c])
            multiply(gtop, c)
            push(gtop.at[c], gin.at[c], s_hop.at[c], r_g.at[c], device(x, y, below, t))

        def step(c, carry):
            pl.when(c + 1 < CHUNKS)(lambda: begin(c + 1))
            pl.when(c == MOVE_AT)(move_inputs)
            add_up(c)
            return carry

        begin(0)
        lax.fori_loop(0, CHUNKS, step, 0)
        wait_bytes(vd, r_w2.at[0])

    @pl.when(z < 7)
    def _():
        move_inputs()
        wait_bytes(vd, r_w2.at[0])
        pl.when(z < 2)(values_stage)

        def step(c, carry):
            add_branch(c)
            multiply(gout, c)
            push(gout.at[c], gin.at[c], s_hop.at[c], r_g.at[c], device(x, y, below, t))
            add_up(c)
            pl.when(z < PACED)(functools.partial(rows_out, c))
            hand_in(c)
            return carry

        lax.fori_loop(0, CHUNKS, step, 0)

    pl.when(z >= 2)(values_stage)

    @pl.when(z == 7)
    def _():
        def step(c, carry):
            add_branch(c)
            hand_out(c)

            @pl.when(c == GO_AT)
            def _():
                for k in range(1, 8):
                    pl.semaphore_signal(
                        go, inc=1, device_id=device(x, y, lax.rem(z + k, 8), t), device_id_type=MESH
                    )

            return carry

        lax.fori_loop(0, CHUNKS, step, 0)

    paced = jnp.logical_and(z >= PACED, z < 7)

    @pl.when(paced)
    def _():
        def step(c, carry):
            rows_out(c)
            for k, src, dst, to in out_parts(c):
                sent(src, s_out.at[c, k], to)
            return carry

        lax.fori_loop(0, CHUNKS, step, 0)

    wait_bytes(xd, r_xd)
    wait_bytes(val.at[pl.ds(0, 3)], r_val)
    wait_bytes(gd, r_gd)
    wait_bytes(vg.at[pl.ds(0, 3)], r_vg)
    accv[...] = jnp.zeros_like(accv)
    acco[...] = jnp.zeros_like(acco)

    def grad_step(j, carry):
        accv[...] += dot(xd[j].reshape(512, 256), vg[j].reshape(512, 512), TN)
        acco[...] += dot(val[j], gd[j].reshape(512, 256), TN)
        return carry

    lax.fori_loop(0, 4, grad_step, 0)
    scale = 1.0 / math.sqrt(2048)
    for t2 in range(2):
        dvb[t2] = (accv[:, t2 * 256 : t2 * 256 + 256] * scale).astype(BF16)
        dob[t2, 0:16, :] = jnp.zeros((16, 256), BF16)
        dob[t2, 16:272, :] = (acco[t2 * 256 : t2 * 256 + 256, :] * scale).astype(BF16)
        dob[t2, 272:288, :] = jnp.zeros((16, 256), BF16)

    owner = 2 * x + t
    place = 8 * x + 4 * t + y
    half = lax.rem(after, 2)

    def mid_parts():
        for t2 in range(2):
            for q in range(2):
                dst = mid.at[lax.div(after, 2), t2]
                yield t2, q, dob.at[t2, pl.ds(128 * q, 160)], dst, device(x, y, 4 * half + 2 + q, t)

    def owner_parts():
        for t2 in range(2):
            main = vwin.at[pl.ds(pl.multiple_of(128 + y * 256, 128), 256)]
            yield t2, 0, dvb.at[t2], main, (after, owner, t2), None
            yield t2, 1, dvb.at[t2, pl.ds(128, 128)], vwin.at[pl.ds(0, 128)], (after, owner + 1, t2), y == 3
            low = jnp.logical_and(y == 0, owner >= 1)
            yield t2, 2, dvb.at[t2, pl.ds(0, 128)], vwin.at[pl.ds(1152, 128)], (after, owner - 1, t2), low
            yield t2, 3, dob.at[t2, pl.ds(16, 16)], owin.at[place, pl.ds(48, 16)], (after, 7, t2), None

    def fin_parts(j):
        for t2 in range(2):
            for y2 in range(4):
                to = (2 * j + zh, zl * 4 + y2, t2)
                yield t2 * 4 + y2, mid.at[j, t2, pl.ds(32 * y2, 64)], owin.at[place], to

    def guarded(cond, what):
        if cond is None:
            what()
        else:
            pl.when(cond)(what)

    @pl.when(z < 7)
    def _():
        pl.semaphore_wait(go, 1)

    for t2, q, src, dst, to in mid_parts():
        send(src, dst, s_mid.at[t2, q], r_mid.at[lax.div(after, 2), t2], to)
    for t2, k, src, dst, to, cond in owner_parts():
        guarded(cond, functools.partial(send, src, dst, s_own.at[t2, k], r_own.at[k], to))

    @pl.when(zl >= 2)
    def _():
        for j in reversed(range(4)):
            for t2 in range(2):
                wait_bytes(mid.at[j, t2], r_mid.at[j, t2])
            for k, src, dst, to in fin_parts(j):
                send(src, dst, s_fin.at[j, k], r_own.at[3], to)

    @pl.when(dp <= 7)
    def _():
        wait_bytes(vwin.at[pl.ds(128, 1024)], r_own.at[0])

    @pl.when(jnp.logical_and(dp >= 1, dp <= 8))
    def _():
        wait_bytes(vwin.at[pl.ds(0, 128)], r_own.at[1])

    @pl.when(dp <= 6)
    def _():
        wait_bytes(vwin.at[pl.ds(1152, 128)], r_own.at[2])

    @pl.when(dp == 7)
    def _():
        wait_bytes(owin.at[pl.ds(0, 8)], r_own.at[3])

    @pl.when(dp >= 8)
    def _():
        wait_bytes(owin, r_own.at[3])

    wait_bytes(out, r_out)

    sent(vw, s_wa.at[0], wa_to)
    sent(ow, s_wa.at[1], wa_to)

    @pl.when(top_sender)
    def _():
        for k, src, dst, c, to in top_parts():
            sent(src, s_top.at[k], to)

    for which in (1, 0):

        @pl.when(x == zl)
        def _():
            for k, src, dst, to in w1_parts(which):
                sent(src, s_w1.at[k, which], to)

        for k, src, dst, to in w2_parts(which):
            sent(src, s_w2.at[k, which], to)
    for k, src, to in x_moves():
        sent(src, s_x.at[k], to)
    for k, src, to in x_parts():
        sent(src, s_xa.at[k], to)
    for k, src, to in xd_parts():
        sent(src, s_xd.at[k], to)
    wait_bytes(rsv, s_rsv)
    wait_bytes(rsv, s_agv)
    for k, y2 in y_peers():
        wait_bytes(val.at[y], s_val.at[k])

    def drain(c, carry):
        wait_bytes(rsb.at[c], s_rs.at[c])
        wait_bytes(vg.at[y, c], s_ag.at[c])
        wait_bytes(gout.at[c], s_hop.at[c])
        for k, src, to in gd_parts(c):
            sent(src, s_gd.at[c, k], to)

        @pl.when(jnp.logical_not(paced))
        def _():
            for k, src, dst, to in out_parts(c):
                sent(src, s_out.at[c, k], to)

        for k, y2 in y_peers():
            wait_bytes(vg.at[y, c], s_vg.at[c, k])
        return carry

    lax.fori_loop(0, CHUNKS, drain, 0)
    for t2, q, src, dst, to in mid_parts():
        sent(src, s_mid.at[t2, q], to)
    for t2, k, src, dst, to, cond in owner_parts():
        guarded(cond, functools.partial(sent, src, s_own.at[t2, k], to))

    @pl.when(zl >= 2)
    def _():
        for j in range(4):
            for k, src, dst, to in fin_parts(j):
                sent(src, s_fin.at[j, k], to)


def relay(xin, top, vw, ow):
    hbm = pl.BlockSpec(memory_space=pl.ANY)
    dma = pltpu.SemaphoreType.DMA
    return pl.pallas_call(
        relay_kernel,
        out_shape=(
            jax.ShapeDtypeStruct((4, 16, 8192), BF16),
            jax.ShapeDtypeStruct((1280, 256), BF16),
            jax.ShapeDtypeStruct((32, 64, 256), BF16),
        ),
        in_specs=[hbm] * 4,
        out_specs=(hbm, hbm, hbm),
        scratch_shapes=[
            pltpu.VMEM((CHUNKS, ROWS, 1024), BF16),
            pltpu.VMEM((CHUNKS, ROWS, 1024), BF16),
            pltpu.VMEM((CHUNKS, ROWS, 1024), BF16),
            pltpu.VMEM((4, 128, 1024), BF16),
            pltpu.VMEM((4, 4, 32, 1024), BF16),
            pltpu.VMEM((4, 512, 256), BF16),
            pltpu.VMEM((4, 256, 512), BF16),
            pltpu.VMEM((512, 256), BF16),
            pltpu.VMEM((256, 512), BF16),
            pltpu.VMEM((1024, 512), BF16),
            pltpu.VMEM((512, 1024), BF16),
            pltpu.VMEM((CHUNKS, ROWS, 512), BF16),
            pltpu.VMEM((CHUNKS, 7, PIECE, 256), BF16),
            pltpu.VMEM((CHUNKS, PIECE, 256), BF16),
            pltpu.VMEM((4, CHUNKS, ROWS, 512), BF16),
            pltpu.VMEM((4, CHUNKS, ROWS, 256), BF16),
            pltpu.VMEM((512, 512), BF16),
            pltpu.VMEM((7, 128, 256), BF16),
            pltpu.VMEM((4, 512, 512), BF16),
            pltpu.VMEM((4, 4, 128, 256), BF16),
            pltpu.VMEM((256, 512), F32),
            pltpu.VMEM((512, 256), F32),
            pltpu.VMEM((2, 256, 256), BF16),
            pltpu.VMEM((2, 288, 256), BF16),
            pltpu.VMEM((4, 2, 160, 256), BF16),
            dma((8,)), dma((4,)), dma((2,)), dma((4, 2)), dma((4, 2)), dma((8,)),
            dma((CHUNKS,)), dma((CHUNKS,)), dma((CHUNKS,)), dma((CHUNKS, ROWS // 16)),
            dma((CHUNKS, 4)), dma((CHUNKS, 3)), dma, dma,
            dma((3,)), dma((4,)), dma((2, 4)), dma((2, 2)), dma((4, 8)),
            dma((4,)), dma, dma((4, 2)), dma((2,)), dma((2,)),
            dma((CHUNKS,)), dma((CHUNKS,)), dma((CHUNKS,)), dma((CHUNKS,)),
            dma, dma, dma, dma, dma, dma,
            dma((4,)), dma((4, 2)), dma, pltpu.SemaphoreType.REGULAR,
        ],
        compiler_params=pltpu.CompilerParams(has_side_effects=True, vmem_limit_bytes=60 * 1024 * 1024),
    )(xin, top, vw, ow)


def adam_kernel(steps, lengths, vwin, owin, param, first, second, new_param, new_first, new_second, flat):
    dp = lax.axis_index("dp")
    step = pl.program_id(0)
    rows = param.shape[0]

    def from_value(low, high):
        for a in range(low, high, 128):
            part = vwin[a : a + 128, :].astype(F32)
            flat[pl.ds(2 * a, 128, stride=2), :] = part[:, :128]
            flat[pl.ds(2 * a + 1, 128, stride=2), :] = part[:, 128:]

    def from_output(low, high):
        for e in range(32):
            part = owin[e].astype(F32)[12 + low : 12 + high, :]
            for h in range(2):
                flat[pl.ds(low * 64 + e * 2 + h, high - low, stride=64), :] = part[:, h * 128 : h * 128 + 128]

    @pl.when(step == 0)
    def _():
        flat[2560:, :] = jnp.zeros((flat.shape[0] - 2560, 128), F32)
        for last, value_rows, output_rows in ((8, (0, 128), (0, 4)), (7, (128, 1152), (4, 36)), (6, (1152, 1280), (36, 40))):
            pl.when(dp <= last)(functools.partial(from_value, *value_rows))
            pl.when(dp > last)(functools.partial(from_output, *output_rows))

    start = lax.fori_loop(0, dp, lambda e, total: total + lengths[e], jnp.int32(0))
    length = lengths[dp]
    offset = start - dp * 262144 + 32768
    row, lane = lax.div(offset, 128), lax.rem(offset, 128)
    window = flat[pl.ds(step * rows + row, rows + 8), :]
    turned = pltpu.roll(window, lax.rem(128 - lane, 128), 1)
    lanes = lax.broadcasted_iota(jnp.int32, (rows, 128), 1)
    grad = jnp.where(lanes < 128 - lane, turned[:rows], turned[1 : rows + 1])
    index = (step * rows + lax.broadcasted_iota(jnp.int32, (rows, 128), 0)) * 128 + lanes
    grad = jnp.where(index < length, grad, 0.0)

    first_new = beta_one * first[...] + (1.0 - beta_one) * grad
    second_new = beta_two * second[...] + (1.0 - beta_two) * grad * grad
    corrected = (
        first_new
        / (1.0 - beta_one**adam_step)
        / (jnp.sqrt(second_new / (1.0 - beta_two**adam_step)) + adam_eps)
    )
    new_param[...] = param[...] - learn_rate * (corrected + decay_rate * param[...])
    new_first[...] = first_new
    new_second[...] = second_new


def adam(lengths, vwin, owin, param, first, second):
    steps = 5
    block = pl.BlockSpec((2560 // steps, 128), lambda i: (i, 0))
    shape = jax.ShapeDtypeStruct((2560, 128), F32)
    return pl.pallas_call(
        functools.partial(adam_kernel, steps),
        grid=(steps,),
        out_shape=(shape, shape, shape),
        in_specs=[
            pl.BlockSpec(memory_space=pltpu.SMEM),
            pl.BlockSpec(memory_space=pltpu.VMEM),
            pl.BlockSpec(memory_space=pltpu.VMEM),
            block,
            block,
            block,
        ],
        out_specs=(block, block, block),
        scratch_shapes=[pltpu.VMEM((2560 + 528, 128), F32)],
        compiler_params=pltpu.CompilerParams(vmem_limit_bytes=32 * 1024 * 1024),
    )(lengths, vwin, owin, param, first, second)


def local(section_inputs, top_grad, value_weight, output_weight, owner_lengths, master_param, moment1, moment2):
    out, vwin, owin = relay(section_inputs[0], top_grad, value_weight[0], output_weight[0])
    flat = (2560, 128)
    updated = adam(
        owner_lengths[0, 0], vwin, owin, master_param.reshape(flat), moment1.reshape(flat), moment2.reshape(flat)
    )
    return (out[None], *(array.reshape(1, 1, -1) for array in updated))


def solution(mesh):
    in_specs = (
        P("section", None, ("dp", "tensor"), None),
        P(None, ("dp", "tensor"), None),
        P("section", "dp", "tensor"),
        P("section", "tensor", "dp"),
        P("section", "tensor", None),
        P("section", "tensor", "dp"),
        P("section", "tensor", "dp"),
        P("section", "tensor", "dp"),
    )
    out_specs = (
        P("section", None, ("dp", "tensor"), None),
        P("section", "tensor", "dp"),
        P("section", "tensor", "dp"),
        P("section", "tensor", "dp"),
    )
    return jax.shard_map(local, mesh=mesh, in_specs=in_specs, out_specs=out_specs, check_vma=False)
```

```python
import functools
import math

import jax
import jax.numpy as jnp
from jax import lax
from jax.experimental import pallas as pl
from jax.experimental.pallas import tpu as pltpu
from jax.sharding import PartitionSpec as P

MESH = pl.DeviceIdType.MESH
BF16 = jnp.bfloat16
F32 = jnp.float32

beta_one = 0.9
beta_two = 0.95
learn_rate = 0.001
decay_rate = 0.1
adam_eps = 1e-08
adam_step = 20.0

CHUNKS = 8
ROWS = 512 // CHUNKS
PIECE = ROWS // 4
PACED = 2
GO_AT = 6
MOVE_AT = 7
NT = (((1,), (1,)), ((), ()))
NN = (((1,), (0,)), ((), ()))
TN = (((0,), (0,)), ((), ()))


def dot(a, b, dims):
    return lax.dot_general(a, b, dims, preferred_element_type=F32)


def device(x, y, z, t):
    return (2 * x + lax.div(z, 4), lax.rem(z, 4) * 4 + y, t)


def aligned(start, size):
    return pl.ds(pl.multiple_of(start, size), size)


def wait_bytes(ref, sem):
    pltpu.make_async_copy(ref, ref, sem).wait()


def relay_kernel(
    xin, top, vw, ow,
    out, vwin, owin,
    gtop, gin, gout, xrow, xst, vwst, owst, vst, ost, vd, od, pbuf, rsb, vgo, vg, gd, pv, rsv, val, xd,
    accv, acco, dvb, dob, mid,
    s_xa, s_x, s_wa, s_w1, s_w2, s_top, s_rs, s_ag, s_hop, s_out, s_gd, s_vg, s_rsv, s_agv, s_val, s_xd,
    s_own, s_mid, s_fin,
    r_xa, r_x, r_wa, r_w1, r_w2, r_top, r_g, r_rs, r_ag, r_gd, r_vg, r_rsv, r_agv, r_val, r_xd, r_own, r_mid, r_out, go,
):
    sec = lax.axis_index("section")
    dp = lax.axis_index("dp")
    t = lax.axis_index("tensor")
    x = lax.div(sec, 2)
    zh = lax.rem(sec, 2)
    zl = lax.div(dp, 4)
    y = lax.rem(dp, 4)
    z = zh * 4 + zl
    after = lax.rem(z + 1, 8)
    below = lax.rem(z + 7, 8)

    def is_me(to):
        return jnp.logical_and(jnp.logical_and(to[0] == sec, to[1] == dp), to[2] == t)

    def send(src, dst, ssem, rsem, to):
        mine = is_me(to)

        @pl.when(mine)
        def _():
            pltpu.make_async_copy(src, dst, rsem).start()

        @pl.when(jnp.logical_not(mine))
        def _():
            pltpu.make_async_remote_copy(src, dst, ssem, rsem, device_id=to, device_id_type=MESH).start()

    def sent(src, ssem, to):
        @pl.when(jnp.logical_not(is_me(to)))
        def _():
            wait_bytes(src, ssem)

    def push(src, dst, ssem, rsem, to):
        pltpu.make_async_remote_copy(src, dst, ssem, rsem, device_id=to, device_id_type=MESH).start()

    wa_to = device(zl, y, z, t)
    send(ow, owst.at[x], s_wa.at[1], r_wa.at[x, 1], wa_to)

    def top_parts():
        for mb in range(4):
            for t2 in range(2):
                row = mb * 128 + zl * 32 + t * 16
                c, rest = lax.div(row, ROWS), lax.rem(row, ROWS)
                src = top.at[mb, :, aligned(x * 2048 + t2 * 1024, 1024)]
                yield mb * 2 + t2, src, gtop.at[c, aligned(rest, 16), :], c, device(x, y, 7, t2)

    top_sender = jnp.logical_or(z < 2, z >= 6)

    @pl.when(top_sender)
    def _():
        for k, src, dst, c, to in top_parts():
            send(src, dst, s_top.at[k], r_top.at[c], to)

    send(vw, vwst.at[x], s_wa.at[0], r_wa.at[x, 0], wa_to)

    def w1_parts(which):
        for x2 in reversed(range(4)):
            plane = 2 * x2 + zh
            if which:
                yield x2, owst.at[x2], ost, device(x, y, plane, t)
            else:
                yield x2, vwst.at[x2], vst, device(x, y, lax.rem(plane + 7, 8), t)

    def w2_parts(which):
        rows = aligned(lax.rem(y, 2) * 512, 512)
        cols = aligned(t * 256, 256)
        for y2 in range(4):
            to = device(x, y2, z, lax.div(y, 2))
            if which:
                yield y2, ost, od.at[cols, rows], to
            else:
                yield y2, vst, vd.at[rows, cols], to

    def x_parts():
        for x2 in range(4):
            for t2 in range(2):
                yield x2 * 2 + t2, xin.at[:, :, pl.ds(x2 * 2048 + t2 * 1024, 1024)], device(x2, y, z, t2)

    def x_moves():
        for x2 in reversed(range(4)):
            yield x2, xst.at[x2], device(x, y, lax.rem(2 * x2 + zh + 7, 8), t)

    def move_inputs():
        for k, src, to in x_moves():
            wait_bytes(src, r_xa.at[k])
            send(src, xrow.at[:, aligned(zl * 32, 32), :], s_x.at[k], r_x, to)

    for which in (1, 0):

        @pl.when(x == zl)
        def _():
            for k, src, dst, to in w1_parts(which):
                wait_bytes(src, r_wa.at[k, which])
                send(src, dst, s_w1.at[k, which], r_w1.at[which], to)

        wait_bytes(ost if which else vst, r_w1.at[which])
        for k, src, dst, to in w2_parts(which):
            send(src, dst, s_w2.at[k, which], r_w2.at[which], to)
    for k, src, to in x_parts():
        send(src, xst.at[x, :, aligned(t * 16, 16), :], s_xa.at[k], r_xa.at[x], to)
    wait_bytes(od, r_w2.at[1])

    def peers():
        for k in range(1, 8):
            yield k - 1, lax.rem(x + k // 2, 4), lax.rem(t + k % 2, 2)

    def y_peers():
        for k in range(1, 4):
            yield k - 1, lax.rem(y + k, 4)

    def multiply(ref, c):
        pbuf[c] = dot(ref[c], od[...], NT).astype(BF16)
        for k, x2, t2 in peers():
            push(
                pbuf.at[c, aligned(x2 * PIECE, PIECE), aligned(t2 * 256, 256)],
                rsb.at[c, k],
                s_rs.at[c],
                r_rs.at[c],
                device(x2, y, z, t2),
            )

    def add_up(c):
        rows, cols = aligned(x * PIECE, PIECE), aligned(t * 256, 256)
        wait_bytes(rsb.at[c], r_rs.at[c])
        total = pbuf[c, rows, cols].astype(F32)
        for k in range(7):
            total = total + rsb[c, k].astype(F32)
        vgo[c] = total.astype(BF16)
        for k in range(8):
            to = device(lax.rem(x + k // 2, 4), y, below, lax.rem(t + k % 2, 2))
            push(vgo.at[c], vg.at[y, c, rows, cols], s_ag.at[c], r_ag.at[c], to)

    def add_branch(c):
        wait_bytes(gin.at[c], r_g.at[c])
        wait_bytes(vg.at[y, c], r_ag.at[c])
        branch = dot(vg[y, c], vd[...], NT)
        gout[c] = (gin[c].astype(F32) + branch).astype(BF16)

    def gd_parts(c):
        for y2 in range(4):
            yield y2, gin.at[c, :, pl.ds(y2 * 256, 256)], device(x, y2, z, t)

    def out_parts(c):
        for a in range(ROWS // 16):
            row = c * ROWS + a * 16
            mb, z2, t2 = lax.div(row, 128), lax.rem(lax.div(row, 32), 4), a % 2
            dst = out.at[mb, :, aligned(x * 2048 + t * 1024, 1024)]
            yield a, gout.at[c, pl.ds(a * 16, 16), :], dst, (after, z2 * 4 + y, t2)

    def rows_out(c):
        for k, src, dst, to in out_parts(c):
            send(src, dst, s_out.at[c, k], r_out, to)

    def hand_out(c):
        rows_out(c)
        hand_in(c)

    def hand_in(c):
        for k, y2 in y_peers():
            push(vg.at[y, c], vg.at[y, c], s_vg.at[c, k], r_vg, device(x, y2, z, t))
        for k, src, to in gd_parts(c):
            send(src, gd.at[y, c], s_gd.at[c, k], r_gd, to)

    def xd_parts():
        for y2 in range(4):
            yield y2, xrow.at[:, :, pl.ds(y2 * 256, 256)], device(x, y2, z, t)

    def values_stage():
        wait_bytes(xrow, r_x)
        for k, src, to in xd_parts():
            send(src, xd.at[y], s_xd.at[k], r_xd, to)

        def block(i, carry):
            pv[aligned(i * 128, 128), :] = dot(xrow[i], vd[...], NN).astype(BF16)
            return carry

        lax.fori_loop(0, 4, block, 0)
        for k, x2, t2 in peers():
            push(
                pv.at[aligned(x2 * 128, 128), aligned(t2 * 256, 256)], rsv.at[k], s_rsv, r_rsv, device(x2, y, z, t2)
            )
        wait_bytes(rsv, r_rsv)
        rows, cols = aligned(x * 128, 128), aligned(t * 256, 256)
        total = pv[rows, cols].astype(F32)
        for k in range(7):
            total = total + rsv[k].astype(F32)
        val[y, rows, cols] = total.astype(BF16)
        mine = val.at[y, rows, cols]
        for k, x2, t2 in peers():
            push(mine, mine, s_agv, r_agv, device(x2, y, z, t2))
        wait_bytes(rsv, r_agv)
        for k, y2 in y_peers():
            push(val.at[y], val.at[y], s_val.at[k], r_val, device(x, y2, z, t))

    @pl.when(z == 7)
    def _():
        def begin(c):
            wait_bytes(gtop.at[c], r_top.at[c])
            multiply(gtop, c)
            push(gtop.at[c], gin.at[c], s_hop.at[c], r_g.at[c], device(x, y, below, t))

        def step(c, carry):
            pl.when(c + 1 < CHUNKS)(lambda: begin(c + 1))
            pl.when(c == MOVE_AT)(move_inputs)
            add_up(c)
            return carry

        begin(0)
        lax.fori_loop(0, CHUNKS, step, 0)
        wait_bytes(vd, r_w2.at[0])

    @pl.when(z < 7)
    def _():
        move_inputs()
        wait_bytes(vd, r_w2.at[0])
        pl.when(z < 2)(values_stage)

        def step(c, carry):
            add_branch(c)
            multiply(gout, c)
            push(gout.at[c], gin.at[c], s_hop.at[c], r_g.at[c], device(x, y, below, t))
            add_up(c)
            pl.when(z < PACED)(functools.partial(rows_out, c))
            hand_in(c)
            return carry

        lax.fori_loop(0, CHUNKS, step, 0)

    pl.when(z >= 2)(values_stage)

    @pl.when(z == 7)
    def _():
        def step(c, carry):
            add_branch(c)
            hand_out(c)

            @pl.when(c == GO_AT)
            def _():
                for k in range(1, 8):
                    pl.semaphore_signal(
                        go, inc=1, device_id=device(x, y, lax.rem(z + k, 8), t), device_id_type=MESH
                    )

            return carry

        lax.fori_loop(0, CHUNKS, step, 0)

    paced = jnp.logical_and(z >= PACED, z < 7)

    @pl.when(paced)
    def _():
        def step(c, carry):
            rows_out(c)
            for k, src, dst, to in out_parts(c):
                sent(src, s_out.at[c, k], to)
            return carry

        lax.fori_loop(0, CHUNKS, step, 0)

    wait_bytes(xd, r_xd)
    wait_bytes(val.at[pl.ds(0, 3)], r_val)
    wait_bytes(gd, r_gd)
    wait_bytes(vg.at[pl.ds(0, 3)], r_vg)
    accv[...] = jnp.zeros_like(accv)
    acco[...] = jnp.zeros_like(acco)

    def grad_step(j, carry):
        accv[...] += dot(xd[j].reshape(512, 256), vg[j].reshape(512, 512), TN)
        acco[...] += dot(val[j], gd[j].reshape(512, 256), TN)
        return carry

    lax.fori_loop(0, 4, grad_step, 0)
    scale = 1.0 / math.sqrt(2048)
    for t2 in range(2):
        dvb[t2] = (accv[:, t2 * 256 : t2 * 256 + 256] * scale).astype(BF16)
        dob[t2, 0:16, :] = jnp.zeros((16, 256), BF16)
        dob[t2, 16:272, :] = (acco[t2 * 256 : t2 * 256 + 256, :] * scale).astype(BF16)
        dob[t2, 272:288, :] = jnp.zeros((16, 256), BF16)

    owner = 2 * x + t
    place = 8 * x + 4 * t + y
    half = lax.rem(after, 2)

    def mid_parts():
        for t2 in range(2):
            for q in range(2):
                dst = mid.at[lax.div(after, 2), t2]
                yield t2, q, dob.at[t2, pl.ds(128 * q, 160)], dst, device(x, y, 4 * half + 2 + q, t)

    def owner_parts():
        for t2 in range(2):
            main = vwin.at[pl.ds(pl.multiple_of(128 + y * 256, 128), 256)]
            yield t2, 0, dvb.at[t2], main, (after, owner, t2), None
            yield t2, 1, dvb.at[t2, pl.ds(128, 128)], vwin.at[pl.ds(0, 128)], (after, owner + 1, t2), y == 3
            low = jnp.logical_and(y == 0, owner >= 1)
            yield t2, 2, dvb.at[t2, pl.ds(0, 128)], vwin.at[pl.ds(1152, 128)], (after, owner - 1, t2), low
            yield t2, 3, dob.at[t2, pl.ds(16, 16)], owin.at[place, pl.ds(48, 16)], (after, 7, t2), None

    def fin_parts(j):
        for t2 in range(2):
            for y2 in range(4):
                to = (2 * j + zh, zl * 4 + y2, t2)
                yield t2 * 4 + y2, mid.at[j, t2, pl.ds(32 * y2, 64)], owin.at[place], to

    def guarded(cond, what):
        if cond is None:
            what()
        else:
            pl.when(cond)(what)

    @pl.when(z < 7)
    def _():
        pl.semaphore_wait(go, 1)

    for t2, q, src, dst, to in mid_parts():
        send(src, dst, s_mid.at[t2, q], r_mid.at[lax.div(after, 2), t2], to)
    for t2, k, src, dst, to, cond in owner_parts():
        guarded(cond, functools.partial(send, src, dst, s_own.at[t2, k], r_own.at[k], to))

    @pl.when(zl >= 2)
    def _():
        for j in reversed(range(4)):
            for t2 in range(2):
                wait_bytes(mid.at[j, t2], r_mid.at[j, t2])
            for k, src, dst, to in fin_parts(j):
                send(src, dst, s_fin.at[j, k], r_own.at[3], to)

    @pl.when(dp <= 7)
    def _():
        wait_bytes(vwin.at[pl.ds(128, 1024)], r_own.at[0])

    @pl.when(jnp.logical_and(dp >= 1, dp <= 8))
    def _():
        wait_bytes(vwin.at[pl.ds(0, 128)], r_own.at[1])

    @pl.when(dp <= 6)
    def _():
        wait_bytes(vwin.at[pl.ds(1152, 128)], r_own.at[2])

    @pl.when(dp == 7)
    def _():
        wait_bytes(owin.at[pl.ds(0, 8)], r_own.at[3])

    @pl.when(dp >= 8)
    def _():
        wait_bytes(owin, r_own.at[3])

    wait_bytes(out, r_out)

    sent(vw, s_wa.at[0], wa_to)
    sent(ow, s_wa.at[1], wa_to)

    @pl.when(top_sender)
    def _():
        for k, src, dst, c, to in top_parts():
            sent(src, s_top.at[k], to)

    for which in (1, 0):

        @pl.when(x == zl)
        def _():
            for k, src, dst, to in w1_parts(which):
                sent(src, s_w1.at[k, which], to)

        for k, src, dst, to in w2_parts(which):
            sent(src, s_w2.at[k, which], to)
    for k, src, to in x_moves():
        sent(src, s_x.at[k], to)
    for k, src, to in x_parts():
        sent(src, s_xa.at[k], to)
    for k, src, to in xd_parts():
        sent(src, s_xd.at[k], to)
    wait_bytes(rsv, s_rsv)
    wait_bytes(rsv, s_agv)
    for k, y2 in y_peers():
        wait_bytes(val.at[y], s_val.at[k])

    def drain(c, carry):
        wait_bytes(rsb.at[c], s_rs.at[c])
        wait_bytes(vg.at[y, c], s_ag.at[c])
        wait_bytes(gout.at[c], s_hop.at[c])
        for k, src, to in gd_parts(c):
            sent(src, s_gd.at[c, k], to)

        @pl.when(jnp.logical_not(paced))
        def _():
            for k, src, dst, to in out_parts(c):
                sent(src, s_out.at[c, k], to)

        for k, y2 in y_peers():
            wait_bytes(vg.at[y, c], s_vg.at[c, k])
        return carry

    lax.fori_loop(0, CHUNKS, drain, 0)
    for t2, q, src, dst, to in mid_parts():
        sent(src, s_mid.at[t2, q], to)
    for t2, k, src, dst, to, cond in owner_parts():
        guarded(cond, functools.partial(sent, src, s_own.at[t2, k], to))

    @pl.when(zl >= 2)
    def _():
        for j in range(4):
            for k, src, dst, to in fin_parts(j):
                sent(src, s_fin.at[j, k], to)


def relay(xin, top, vw, ow):
    hbm = pl.BlockSpec(memory_space=pl.ANY)
    dma = pltpu.SemaphoreType.DMA
    return pl.pallas_call(
        relay_kernel,
        out_shape=(
            jax.ShapeDtypeStruct((4, 16, 8192), BF16),
            jax.ShapeDtypeStruct((1280, 256), BF16),
            jax.ShapeDtypeStruct((32, 64, 256), BF16),
        ),
        in_specs=[hbm] * 4,
        out_specs=(hbm, hbm, hbm),
        scratch_shapes=[
            pltpu.VMEM((CHUNKS, ROWS, 1024), BF16),
            pltpu.VMEM((CHUNKS, ROWS, 1024), BF16),
            pltpu.VMEM((CHUNKS, ROWS, 1024), BF16),
            pltpu.VMEM((4, 128, 1024), BF16),
            pltpu.VMEM((4, 4, 32, 1024), BF16),
            pltpu.VMEM((4, 512, 256), BF16),
            pltpu.VMEM((4, 256, 512), BF16),
            pltpu.VMEM((512, 256), BF16),
            pltpu.VMEM((256, 512), BF16),
            pltpu.VMEM((1024, 512), BF16),
            pltpu.VMEM((512, 1024), BF16),
            pltpu.VMEM((CHUNKS, ROWS, 512), BF16),
            pltpu.VMEM((CHUNKS, 7, PIECE, 256), BF16),
            pltpu.VMEM((CHUNKS, PIECE, 256), BF16),
            pltpu.VMEM((4, CHUNKS, ROWS, 512), BF16),
            pltpu.VMEM((4, CHUNKS, ROWS, 256), BF16),
            pltpu.VMEM((512, 512), BF16),
            pltpu.VMEM((7, 128, 256), BF16),
            pltpu.VMEM((4, 512, 512), BF16),
            pltpu.VMEM((4, 4, 128, 256), BF16),
            pltpu.VMEM((256, 512), F32),
            pltpu.VMEM((512, 256), F32),
            pltpu.VMEM((2, 256, 256), BF16),
            pltpu.VMEM((2, 288, 256), BF16),
            pltpu.VMEM((4, 2, 160, 256), BF16),
            dma((8,)), dma((4,)), dma((2,)), dma((4, 2)), dma((4, 2)), dma((8,)),
            dma((CHUNKS,)), dma((CHUNKS,)), dma((CHUNKS,)), dma((CHUNKS, ROWS // 16)),
            dma((CHUNKS, 4)), dma((CHUNKS, 3)), dma, dma,
            dma((3,)), dma((4,)), dma((2, 4)), dma((2, 2)), dma((4, 8)),
            dma((4,)), dma, dma((4, 2)), dma((2,)), dma((2,)),
            dma((CHUNKS,)), dma((CHUNKS,)), dma((CHUNKS,)), dma((CHUNKS,)),
            dma, dma, dma, dma, dma, dma,
            dma((4,)), dma((4, 2)), dma, pltpu.SemaphoreType.REGULAR,
        ],
        compiler_params=pltpu.CompilerParams(has_side_effects=True, vmem_limit_bytes=60 * 1024 * 1024),
    )(xin, top, vw, ow)


def adam_kernel(steps, lengths, vwin, owin, param, first, second, new_param, new_first, new_second, flat):
    dp = lax.axis_index("dp")
    step = pl.program_id(0)
    rows = param.shape[0]

    def from_value(low, high):
        for a in range(low, high, 128):
            part = vwin[a : a + 128, :].astype(F32)
            flat[pl.ds(2 * a, 128, stride=2), :] = part[:, :128]
            flat[pl.ds(2 * a + 1, 128, stride=2), :] = part[:, 128:]

    def from_output(low, high):
        for e in range(32):
            part = owin[e].astype(F32)[12 + low : 12 + high, :]
            for h in range(2):
                flat[pl.ds(low * 64 + e * 2 + h, high - low, stride=64), :] = part[:, h * 128 : h * 128 + 128]

    @pl.when(step == 0)
    def _():
        flat[2560:, :] = jnp.zeros((flat.shape[0] - 2560, 128), F32)
        for last, value_rows, output_rows in ((8, (0, 128), (0, 4)), (7, (128, 1152), (4, 36)), (6, (1152, 1280), (36, 40))):
            pl.when(dp <= last)(functools.partial(from_value, *value_rows))
            pl.when(dp > last)(functools.partial(from_output, *output_rows))

    start = lax.fori_loop(0, dp, lambda e, total: total + lengths[e], jnp.int32(0))
    length = lengths[dp]
    offset = start - dp * 262144 + 32768
    row, lane = lax.div(offset, 128), lax.rem(offset, 128)
    window = flat[pl.ds(step * rows + row, rows + 8), :]
    turned = pltpu.roll(window, lax.rem(128 - lane, 128), 1)
    lanes = lax.broadcasted_iota(jnp.int32, (rows, 128), 1)
    grad = jnp.where(lanes < 128 - lane, turned[:rows], turned[1 : rows + 1])
    index = (step * rows + lax.broadcasted_iota(jnp.int32, (rows, 128), 0)) * 128 + lanes
    grad = jnp.where(index < length, grad, 0.0)

    first_new = beta_one * first[...] + (1.0 - beta_one) * grad
    second_new = beta_two * second[...] + (1.0 - beta_two) * grad * grad
    corrected = (
        first_new
        / (1.0 - beta_one**adam_step)
        / (jnp.sqrt(second_new / (1.0 - beta_two**adam_step)) + adam_eps)
    )
    new_param[...] = param[...] - learn_rate * (corrected + decay_rate * param[...])
    new_first[...] = first_new
    new_second[...] = second_new


def adam(lengths, vwin, owin, param, first, second):
    steps = 5
    block = pl.BlockSpec((2560 // steps, 128), lambda i: (i, 0))
    shape = jax.ShapeDtypeStruct((2560, 128), F32)
    return pl.pallas_call(
        functools.partial(adam_kernel, steps),
        grid=(steps,),
        out_shape=(shape, shape, shape),
        in_specs=[
            pl.BlockSpec(memory_space=pltpu.SMEM),
            pl.BlockSpec(memory_space=pltpu.VMEM),
            pl.BlockSpec(memory_space=pltpu.VMEM),
            block,
            block,
            block,
        ],
        out_specs=(block, block, block),
        scratch_shapes=[pltpu.VMEM((2560 + 528, 128), F32)],
        compiler_params=pltpu.CompilerParams(vmem_limit_bytes=32 * 1024 * 1024),
    )(lengths, vwin, owin, param, first, second)


def local(section_inputs, top_grad, value_weight, output_weight, owner_lengths, master_param, moment1, moment2):
    out, vwin, owin = relay(section_inputs[0], top_grad, value_weight[0], output_weight[0])
    flat = (2560, 128)
    updated = adam(
        owner_lengths[0, 0], vwin, owin, master_param.reshape(flat), moment1.reshape(flat), moment2.reshape(flat)
    )
    return (out[None], *(array.reshape(1, 1, -1) for array in updated))


def solution(mesh):
    in_specs = (
        P("section", None, ("dp", "tensor"), None),
        P(None, ("dp", "tensor"), None),
        P("section", "dp", "tensor"),
        P("section", "tensor", "dp"),
        P("section", "tensor", None),
        P("section", "tensor", "dp"),
        P("section", "tensor", "dp"),
        P("section", "tensor", "dp"),
    )
    out_specs = (
        P("section", None, ("dp", "tensor"), None),
        P("section", "tensor", "dp"),
        P("section", "tensor", "dp"),
        P("section", "tensor", "dp"),
    )
    return jax.shard_map(local, mesh=mesh, in_specs=in_specs, out_specs=out_specs, check_vma=False)
```
